128 devices in a mesh: node: 8 (over x, core), rail: 16 (over z, y).
Axes of the slice: x: 4, y: 4, z: 4, core: 2. Of those that a mesh axis runs over, the one named last changes fastest.
Arguments:
- tokens: bfloat16 [8192, 2048], P(('node', 'rail')), may hold values from -6 to 6
- routes: int32 [8192, 8], P(('node', 'rail')), may hold values from 0 to 127, all different within a row; in each aligned block of 64 rows (0 to 63, 64 to 127, ...) at most 8 rows name the same one
- route_weights: float32 [8192, 8], P(('node', 'rail')), may hold values from 0.03 to 0.4
- cotangent: bfloat16 [8192, 2048], P(('node', 'rail')), may hold values from -6 to 6
- gate_weight: bfloat16 [128, 2048, 768], P(('node', 'rail')), may hold values from -0.125 to 0.125
- up_weight: bfloat16 [128, 2048, 768], P(('node', 'rail')), may hold values from -0.125 to 0.125
- down_weight: bfloat16 [128, 768, 2048], P(('node', 'rail')), may hold values from -0.21875 to 0.21875
Outputs:
- mixed: bfloat16 [8192, 2048], P(('node', 'rail'))
- token_grad: bfloat16 [8192, 2048], P(('node', 'rail'))
- weight_grad: float32 [8192, 8], P(('node', 'rail'))
- gate_grad: bfloat16 [128, 2048, 768], P(('node', 'rail'))
- up_grad: bfloat16 [128, 2048, 768], P(('node', 'rail'))
- down_grad: bfloat16 [128, 768, 2048], P(('node', 'rail'))
The draws below stay inside these ranges and needn't reach their ends.
Inputs may be any that keep to these rules, and one draw needn't show every extreme that they name: `routes`: each token names 8 different experts. Among the tokens of one block of 64 consecutive tokens no expert is named more than 8 times, and in every draw some expert is named exactly 8 times by one block.
All inputs are finite; a program needn't handle non-finite values.
Results may differ from the reference program's by a relative error of at most 0.0064.
Values may be sent and summed in bfloat16 or wider, within the bound.
A program may use at most 128 MiB of HBM per device.

```python
import math
import jax
import jax.numpy as jnp
import numpy as np
from jax import lax

D = 2048
FF = 768
TOP = 8
TOK_DEV = 64
EXPERTS = 128
TOKENS = 8192
MOST = 8
N_NODE = 8
N_RAIL = 16


def steps_of(own_key, shape, cuts, low, high):
    level, own = 1.0, jax.random.fold_in(own_key, 6)
    for dim, shards_of in cuts:
        draws = jnp.exp(jax.random.uniform(jax.random.fold_in(own, dim), (shards_of,), jnp.float32, low / len(cuts), high / len(cuts)))
        level = level * jnp.repeat(draws, shape[dim] // shards_of).reshape([-1 if axis == dim else 1 for axis in range(len(shape))])
    return level


def shared_out(rng, own, number, rows, number_of, top, limit, lean):
    sequence = jax.random.permutation(rng, number_of)
    heavy_load, ordinary = shares(number_of, rows * top, limit, lean, True), shares(number_of, rows * top, limit, lean, False)
    places = jnp.arange(number_of)

    def named(sizes, turn):
        used = int((sizes > 0).sum())
        fixed = max(1, used // 4)
        shifted = fixed + (places - fixed + turn * (used - fixed)) % max(1, number_of - fixed)
        return jnp.zeros((number_of,), jnp.int32).at[sequence[jnp.where(places < fixed, places, shifted)]].set(jnp.asarray(sizes, jnp.int32))

    sizes = jnp.where(number % 4 == 0, named(heavy_load, number // 4), named(ordinary, number - number // 4 - 1))
    mixed = jax.random.permutation(jax.random.fold_in(own, 3), number_of)
    donor, taker = mixed[0:number_of // 2 * 2:2], mixed[1:number_of // 2 * 2:2]
    margin = jnp.minimum(sizes[donor] - 1, limit - sizes[taker]) // 2
    margin = jnp.where((donor == sequence[0]) | (taker == sequence[0]) | (sizes[taker] == 0), 0, jnp.maximum(margin, 0))
    shifted = jax.random.randint(jax.random.fold_in(own, 4), (number_of // 2,), 0, 1 << 20) % (margin + 1)
    sizes = sizes.at[donor].add(-shifted).at[taker].add(shifted)
    members = jnp.searchsorted(jnp.cumsum(sizes), jnp.arange(rows * top), side="right").astype(jnp.int32)
    table = members.reshape(top, rows).T
    table = table[jax.random.permutation(jax.random.fold_in(own, 1), rows)]
    turn = jax.random.randint(jax.random.fold_in(own, 2), (rows, 1), 0, top)
    return jnp.take_along_axis(table, (jnp.arange(top)[None, :] + turn) % top, axis=1)


def shares(number_of, total, most, lean, full):
    weights = [(1 << 20) // math.isqrt(rank ** lean) + 1 for rank in range(1, number_of + 1)]
    largest = most if full else min(most, max(-(-total // number_of), total * weights[0] // sum(weights)))
    least = 1 if total - largest >= number_of - 1 else 0
    holding, surplus = [largest] + [least] * (number_of - 1), total - largest - least * (number_of - 1)
    while surplus > 0:
        free = [i for i in range(1, number_of) if holding[i] < largest] or [i for i in range(1, number_of) if holding[i] < most]
        mass, left = sum([weights[i] for i in free]), surplus
        for i in free:
            more = min(most - holding[i], max(1, left * weights[i] // mass), surplus)
            holding[i] = holding[i] + more
            surplus = surplus - more
    return np.array(holding)


def noise(key, dims, spread, reach, pieces=(), kind=jnp.bfloat16):
    values = spread * jax.random.normal(key, dims, jnp.float32)
    if pieces:
        values = values * steps_of(key, dims, pieces, -0.22, 0.18)
    return jnp.clip(values, -reach, reach).astype(kind)


def setup_inputs(seed: int = 0) -> dict:
    keys = jax.random.split(jax.random.key(seed), 8)
    tokens = noise(keys[0], (TOKENS, D), 1.0, 6.0, ((0, 128),))
    routes_keys = jax.random.split(jax.random.fold_in(keys[1], 1), TOKENS // TOK_DEV)
    routes_turns = jax.random.permutation(jax.random.fold_in(keys[1], 3), TOKENS // TOK_DEV)
    routes = jax.vmap(lambda own, number: shared_out(jax.random.fold_in(keys[1], 2), own, number, TOK_DEV, EXPERTS, TOP, MOST, 2))(routes_keys, routes_turns).reshape((TOKENS, TOP))
    route_weights = jnp.clip(jnp.exp(math.log(0.4) - 2.5902672 * jax.random.uniform(keys[2], (TOKENS, TOP), jnp.float32) ** steps_of(keys[2], (TOKENS, TOP), ((0, 128),), -0.2, 0.2)), 0.03, 0.4)
    cotangent = noise(keys[3], (TOKENS, D), 1.0, 6.0, ((0, 128),))
    gate_weight = noise(keys[4], (EXPERTS, D, FF), D ** -0.5, 0.125, ((0, 128),))
    up_weight = noise(keys[5], (EXPERTS, D, FF), D ** -0.5, 0.125, ((0, 128),))
    down_weight = noise(keys[6], (EXPERTS, FF, D), FF ** -0.5, 0.21875, ((0, 128),))
    return {"tokens": tokens, "routes": routes, "route_weights": route_weights, "cotangent": cotangent, "gate_weight": gate_weight, "up_weight": up_weight, "down_weight": down_weight}


def expert_forward(slot_rows, w_gate, w_up, w_down):
    gate_pre = jnp.dot(slot_rows, w_gate, preferred_element_type=jnp.float32)
    up_pre = jnp.dot(slot_rows, w_up, preferred_element_type=jnp.float32)
    hidden = (jax.nn.silu(gate_pre) * up_pre).astype(jnp.bfloat16)
    output = jnp.dot(hidden, w_down, preferred_element_type=jnp.float32).astype(jnp.bfloat16)
    return gate_pre, up_pre, hidden, output


def expert_backward(slot_rows, slot_grads, gate_pre, up_pre, hidden, w_gate, w_up, w_down):
    contract_last = (((1,), (1,)), ((), ()))
    contract_first = (((0,), (0,)), ((), ()))
    hidden_back = lax.dot_general(slot_grads, w_down, contract_last, preferred_element_type=jnp.float32)
    sigmoid_gate = jax.nn.sigmoid(gate_pre)
    gate_back = (hidden_back * up_pre * sigmoid_gate * (1.0 + gate_pre * (1.0 - sigmoid_gate))).astype(jnp.bfloat16)
    up_back = (hidden_back * gate_pre * sigmoid_gate).astype(jnp.bfloat16)
    down_grad = lax.dot_general(hidden, slot_grads, contract_first, preferred_element_type=jnp.float32).astype(jnp.bfloat16)
    gate_grad = lax.dot_general(slot_rows, gate_back, contract_first, preferred_element_type=jnp.float32).astype(jnp.bfloat16)
    up_grad = lax.dot_general(slot_rows, up_back, contract_first, preferred_element_type=jnp.float32).astype(jnp.bfloat16)
    input_back = lax.dot_general(gate_back, w_gate, contract_last, preferred_element_type=jnp.float32)
    input_back = input_back + lax.dot_general(up_back, w_up, contract_last, preferred_element_type=jnp.float32)
    return input_back.astype(jnp.bfloat16), gate_grad, up_grad, down_grad


def combine_slots(out_slot, back_slot, route_weights, cotangent):
    out_float = out_slot.astype(jnp.float32)
    mixed = jnp.einsum("tk,tkd->td", route_weights, out_float, precision=lax.Precision.HIGHEST).astype(jnp.bfloat16)
    weight_grad = jnp.einsum("tkd,td->tk", out_float, cotangent.astype(jnp.float32), precision=lax.Precision.HIGHEST)
    token_grad = jnp.sum(back_slot.astype(jnp.float32), axis=1).astype(jnp.bfloat16)
    return mixed, token_grad, weight_grad


def reference(tokens, routes, route_weights, cotangent, gate_weight, up_weight, down_weight):
    blocks = N_NODE * N_RAIL
    flat_routes = routes.reshape(blocks, TOK_DEV * TOP)
    onehot = (flat_routes[:, :, None] == jnp.arange(EXPERTS, dtype=jnp.int32)[None, None, :]).astype(jnp.int32)
    position = jnp.sum((jnp.cumsum(onehot, axis=1) - onehot) * onehot, axis=2)
    source_index = jnp.arange(blocks, dtype=jnp.int32)[:, None]
    slot_index = (flat_routes * (blocks * MOST) + source_index * MOST + position).reshape(-1).astype(jnp.int32)
    total_slots = EXPERTS * blocks * MOST
    owner_row = jnp.zeros((total_slots,), jnp.int32).at[slot_index].set(jnp.arange(TOKENS * TOP, dtype=jnp.int32))
    filled = jnp.zeros((total_slots,), jnp.int32).at[slot_index].set(jnp.ones((TOKENS * TOP,), jnp.int32))
    token_of = (owner_row // TOP).astype(jnp.int32)
    weight_of = route_weights.reshape(-1)[owner_row]

    def one_expert(expert_items):
        w_gate, w_up, w_down, token_rows, weight_rows, live_flag = expert_items
        keep_mask = (live_flag > 0)[:, None]
        slot_rows = jnp.where(keep_mask, tokens[token_rows], jnp.zeros((), jnp.bfloat16))
        slot_grads = jnp.where(keep_mask, weight_rows[:, None] * cotangent[token_rows].astype(jnp.float32), jnp.float32(0.0)).astype(jnp.bfloat16)
        gate_pre, up_pre, hidden, output = expert_forward(slot_rows, w_gate, w_up, w_down)
        input_back, gate_grad, up_grad, down_grad = expert_backward(slot_rows, slot_grads, gate_pre, up_pre, hidden, w_gate, w_up, w_down)
        return output, input_back, gate_grad, up_grad, down_grad

    per_expert = blocks * MOST
    outputs, input_backs, gate_grad, up_grad, down_grad = lax.map(one_expert, (gate_weight, up_weight, down_weight, token_of.reshape(EXPERTS, per_expert), weight_of.reshape(EXPERTS, per_expert), filled.reshape(EXPERTS, per_expert)))
    out_slot = outputs.reshape(-1, D)[slot_index].reshape(TOKENS, TOP, D)
    back_slot = input_backs.reshape(-1, D)[slot_index].reshape(TOKENS, TOP, D)
    mixed, token_grad, weight_grad = combine_slots(out_slot, back_slot, route_weights, cotangent)
    return mixed, token_grad, weight_grad, gate_grad, up_grad, down_grad
```

```python
import jax
import jax.numpy as jnp
from jax import lax
from jax.experimental import pallas as pl
from jax.experimental.pallas import tpu as pltpu
from jax.sharding import PartitionSpec as P

MESH = pl.DeviceIdType.MESH
F32, BF16 = jnp.float32, jnp.bfloat16
PARTS = ((0, 1, 2, 0, 768), (1, 2, 0, 768, 640), (2, 0, 1, 1408, 640))


def place():
    node, rail = lax.axis_index("node"), lax.axis_index("rail")
    return (node // 2, rail % 4, rail // 4), node % 2


def moved(co, axis, value):
    return tuple(value if i == axis else v for i, v in enumerate(co))


def device(co, core):
    return (co[0] * 2 + core, co[2] * 4 + co[1])


def remote(src, dst, send, recv, target):
    return pltpu.make_async_remote_copy(
        src_ref=src, dst_ref=dst, send_sem=send, recv_sem=recv, device_id=target, device_id_type=MESH
    )


def greet(co, core):
    barrier = pltpu.get_barrier_semaphore()
    targets = [device(co, 1 - core)]
    for axis in range(3):
        for step in (1, 2, 3):
            there = moved(co, axis, (co[axis] + step) % 4)
            targets += [device(there, core), device(there, 1 - core)]
    for target in targets:
        pl.semaphore_signal(barrier, inc=1, device_id=target, device_id_type=MESH)
    return barrier, len(targets)


def route_tables(routes, weights):
    lanes = lax.broadcasted_iota(jnp.int32, (64, 128), 1)
    named = jnp.zeros((64, 128), F32)
    for k in range(8):
        named = named + jnp.where(routes[:, k : k + 1] == lanes, 1.0, 0.0)
    row = lax.broadcasted_iota(jnp.int32, (64, 64), 0)
    col = lax.broadcasted_iota(jnp.int32, (64, 64), 1)
    upto = jnp.where(col <= row, 1.0, 0.0).astype(BF16)
    counted = jnp.dot(upto, named.astype(BF16), preferred_element_type=F32)
    table = (counted * named).astype(BF16)
    extra = jnp.zeros((64, 128), F32)
    for k in range(8):
        w = weights[:, k : k + 1]
        high = w.astype(BF16).astype(F32)
        mid = (w - high).astype(BF16).astype(F32)
        low = w - high - mid
        extra = jnp.where(lanes == k, (routes[:, k : k + 1] + 1).astype(F32), extra)
        extra = jnp.where(lanes == 8 + k, high, extra)
        extra = jnp.where(lanes == 16 + k, mid, extra)
        extra = jnp.where(lanes == 24 + k, low, extra)
    return table, extra.astype(BF16)


def one_hot(table, co, slot_axis):
    expert = lax.broadcasted_iota(jnp.int32, (128, 256), 0)
    lane = lax.broadcasted_iota(jnp.int32, (128, 256), 1)
    core, along = lane // 128, (lane // 32) % 4
    there = moved(co, slot_axis, along)
    owner = (there[0] * 2 + core) * 16 + there[2] * 4 + there[1]
    spread = jnp.dot(table, jnp.where(expert == owner, 1.0, 0.0).astype(BF16), preferred_element_type=F32)
    row = lax.broadcasted_iota(jnp.int32, (256, 256), 0)
    lane = lax.broadcasted_iota(jnp.int32, (256, 256), 1)
    wanted = jnp.where(row // 64 == (lane // 8) % 4, lane % 8 + 1, -1).astype(F32)
    return jnp.where(spread == wanted, 1.0, 0.0).astype(BF16)


def dispatch_kernel(tok, cot, routes, weights, *refs):
    xo, co_, rwo, st = refs[0:3], refs[3:6], refs[6], refs[7]
    xb, cb, qb, rwb = refs[8:11], refs[11:14], refs[14:17], refs[17]
    xs, cs, rws = refs[18:21], refs[21:24], refs[24]
    s1, r1, s2, r2, s3, r3, loc = refs[25:32]
    co, core = place()
    barrier, count = greet(co, core)
    table, extra = route_tables(routes[...], weights[...])
    for p, (a1, a2, _, c0, cols) in enumerate(PARTS):
        xb[p][co[a2], co[a1]] = tok[:, c0 : c0 + cols]
        cb[p][co[a2], co[a1]] = cot[:, c0 : c0 + cols]
        qb[p][co[a2], co[a1]] = table
    rwb[co[1], co[0]] = extra
    pl.semaphore_wait(barrier, count)

    tables = [(qb[p], p, p) for p in range(3)] + [(rwb, 0, 3)]
    rows = [(xb[p], p, 4 + p) for p in range(3)]
    grads = [(cb[p], p, 7 + p) for p in range(3)]

    def first_copies(buf, p, n):
        a1, a2 = PARTS[p][:2]
        mine = buf.at[co[a2], co[a1]]
        return [
            remote(mine, mine, s1.at[n, d - 1], r1.at[n, co[a1]], device(moved(co, a1, (co[a1] + d) % 4), core))
            for d in (1, 2, 3)
        ]

    def first_wait(buf, p, n):
        a1, a2 = PARTS[p][:2]
        for d in (1, 2, 3):
            i = (co[a1] + d) % 4
            got = buf.at[co[a2], i]
            remote(got, got, s1.at[n, d - 1], r1.at[n, i], device(moved(co, a1, i), core)).wait_recv()

    def half(buf, block, h):
        return buf.at[block, pl.ds(2 * h, 2)]

    def second_copy(buf, p, n, block, h, right, number):
        a2 = PARTS[p][1]
        part = half(buf, block, h)
        target = device(moved(co, a2, (co[a2] + (1 if right else 3)) % 4), core)
        return remote(part, part, s2.at[n, number], r2.at[n, block, h], target)

    def second_first(buf, p, n):
        me = co[PARTS[p][1]]
        return [
            second_copy(buf, p, n, me, 0, True, 0),
            second_copy(buf, p, n, me, 1, False, 1),
            second_copy(buf, p, n, me, 1, True, 2),
            second_copy(buf, p, n, me, 0, False, 3),
        ]

    def second_wait(buf, p, n, d, h):
        a2 = PARTS[p][1]
        block = (co[a2] + d) % 4
        second_copy(buf, p, n, block, h, True, 0).wait_recv()

    def relay(buf, p, n):
        a2 = PARTS[p][1]
        second_wait(buf, p, n, 3, 0)
        a = second_copy(buf, p, n, (co[a2] + 3) % 4, 0, True, 4)
        a.start()
        second_wait(buf, p, n, 1, 1)
        b = second_copy(buf, p, n, (co[a2] + 1) % 4, 1, False, 5)
        b.start()
        return [a, b]

    def rest_wait(buf, p, n):
        second_wait(buf, p, n, 3, 1)
        second_wait(buf, p, n, 1, 0)
        second_wait(buf, p, n, 2, 0)
        second_wait(buf, p, n, 2, 1)

    sent = []

    def start(copies):
        for c in copies:
            c.start()
        sent.extend(copies)

    for item in tables + rows + grads:
        start(first_copies(*item))
    for item in tables + rows:
        first_wait(*item)
        start(second_first(*item))
    for item in grads:
        first_wait(*item)
        start(second_first(*item))
    for item in tables + rows:
        sent.extend(relay(*item))
    for item in tables:
        rest_wait(*item)
    for p, (_, _, slot_axis, _, _) in enumerate(PARTS):

        def build(g, _, p=p, slot_axis=slot_axis):
            st[p, g] = one_hot(qb[p][g].reshape(256, 128), co, slot_axis)
            return 0

        lax.fori_loop(0, 4, build, 0)

    def pick(buf, out, p):
        cols = buf.shape[-1]

        def step(g, _):
            r = lax.dot_general(
                st[p, g], buf[g].reshape(256, cols), (((0,), (0,)), ((), ())), preferred_element_type=F32
            )
            out[:, pl.ds(pl.multiple_of(g * 32, 32), 32), :] = r.astype(BF16).reshape(8, 32, cols)
            return 0

        lax.fori_loop(0, 4, step, 0)

    def slot_copies(src, dst, p, n):
        axis = PARTS[p][2]
        me = core * 4 + co[axis]
        remotes = []
        for dc in (0, 1):
            for d in (1, 3, 2, 0):
                if dc == 0 and d == 0:
                    continue
                there, other = (co[axis] + d) % 4, (core + dc) % 2
                k = other * 4 + there
                remotes.append(
                    remote(src.at[k], dst.at[me], s3.at[n, dc * 4 + d], r3.at[n, me], device(moved(co, axis, there), other))
                )
        return remotes, pltpu.make_async_copy(src.at[me], dst.at[me], loc.at[n])

    def slot_wait(src, dst, p, n):
        axis = PARTS[p][2]
        for dc in (0, 1):
            for d in (1, 3, 2, 0):
                if dc == 0 and d == 0:
                    continue
                there, other = (co[axis] + d) % 4, (core + dc) % 2
                k = other * 4 + there
                remote(src.at[k], dst.at[k], s3.at[n, dc * 4 + d], r3.at[n, k], device(moved(co, axis, there), other)).wait_recv()

    slots = []

    def send(src, dst, p, n):
        remotes, local = slot_copies(src, dst, p, n)
        start(remotes)
        local.start()
        slots.append((src, dst, p, n, local))

    pick(rwb, rws, 0)
    send(rws, rwo, 0, 0)
    for p in range(3):
        rest_wait(*rows[p])
        pick(xb[p], xs[p], p)
        send(xs[p], xo[p], p, 1 + p)
    for item in grads:
        sent.extend(relay(*item))
    for p in range(3):
        rest_wait(*grads[p])
        pick(cb[p], cs[p], p)
        send(cs[p], co_[p], p, 4 + p)
    for src, dst, p, n, local in slots:
        slot_wait(src, dst, p, n)
        local.wait()
    for c in sent:
        c.wait_send()


def dispatch(tokens, cotangent, routes, weights):
    widths = [part[4] for part in PARTS]
    outs = (
        [jax.ShapeDtypeStruct((8, 128, w), BF16) for w in widths] * 2
        + [jax.ShapeDtypeStruct((8, 128, 128), BF16), jax.ShapeDtypeStruct((3, 4, 256, 256), BF16)]
    )
    any_, vmem = pl.BlockSpec(memory_space=pl.ANY), pl.BlockSpec(memory_space=pltpu.VMEM)
    gathered = [pltpu.VMEM((4, 4, 64, w), BF16) for w in widths]
    table = pltpu.VMEM((4, 4, 64, 128), BF16)
    sends = [pltpu.VMEM((8, 128, w), BF16) for w in widths]
    dma = pltpu.SemaphoreType.DMA
    return pl.pallas_call(
        dispatch_kernel,
        out_shape=outs,
        in_specs=[vmem] * 4,
        out_specs=[any_] * 7 + [vmem],
        scratch_shapes=gathered * 2 + [table] * 4 + sends * 2 + [pltpu.VMEM((8, 128, 128), BF16)]
        + [dma((10, 3)), dma((10, 4)), dma((10, 6)), dma((10, 4, 2)), dma((7, 8)), dma((7, 8)), dma((7,))],
        compiler_params=pltpu.CompilerParams(
            collective_id=0, has_side_effects=True, vmem_limit_bytes=56 * 2**20
        ),
    )(tokens, cotangent, routes, weights)


def expert_forward(slot_rows, w_gate, w_up, w_down):
    gate_pre = jnp.dot(slot_rows, w_gate, preferred_element_type=jnp.float32)
    up_pre = jnp.dot(slot_rows, w_up, preferred_element_type=jnp.float32)
    hidden = (jax.nn.silu(gate_pre) * up_pre).astype(jnp.bfloat16)
    output = jnp.dot(hidden, w_down, preferred_element_type=jnp.float32).astype(jnp.bfloat16)
    return (gate_pre, up_pre, hidden, output)


def expert_backward(slot_rows, slot_grads, gate_pre, up_pre, hidden, w_gate, w_up, w_down):
    contract_last = (((1,), (1,)), ((), ()))
    contract_first = (((0,), (0,)), ((), ()))
    hidden_back = lax.dot_general(
        slot_grads, w_down, contract_last, preferred_element_type=jnp.float32
    )
    sigmoid_gate = jax.nn.sigmoid(gate_pre)
    gate_back = (
        hidden_back * up_pre * sigmoid_gate * (1.0 + gate_pre * (1.0 - sigmoid_gate))
    ).astype(jnp.bfloat16)
    up_back = (hidden_back * gate_pre * sigmoid_gate).astype(jnp.bfloat16)
    down_grad = lax.dot_general(
        hidden, slot_grads, contract_first, preferred_element_type=jnp.float32
    ).astype(jnp.bfloat16)
    gate_grad = lax.dot_general(
        slot_rows, gate_back, contract_first, preferred_element_type=jnp.float32
    ).astype(jnp.bfloat16)
    up_grad = lax.dot_general(
        slot_rows, up_back, contract_first, preferred_element_type=jnp.float32
    ).astype(jnp.bfloat16)
    input_back = lax.dot_general(
        gate_back, w_gate, contract_last, preferred_element_type=jnp.float32
    )
    input_back = input_back + lax.dot_general(
        up_back, w_up, contract_last, preferred_element_type=jnp.float32
    )
    return (input_back.astype(jnp.bfloat16), gate_grad, up_grad, down_grad)


def combine_slots(out_slot, back_slot, route_weights, cotangent):
    out_float = out_slot.astype(jnp.float32)
    mixed = jnp.einsum(
        "tk,tkd->td", route_weights, out_float, precision=lax.Precision.HIGHEST
    ).astype(jnp.bfloat16)
    weight_grad = jnp.einsum(
        "tkd,td->tk", out_float, cotangent.astype(jnp.float32), precision=lax.Precision.HIGHEST
    )
    token_grad = jnp.sum(back_slot.astype(jnp.float32), axis=1).astype(jnp.bfloat16)
    return (mixed, token_grad, weight_grad)


def canonical(parts):
    a, b, c = parts
    w = [part[4] for part in PARTS]
    a = a.reshape(2, 4, 4, 4, 8, w[0]).transpose(3, 0, 1, 2, 4, 5)
    b = b.reshape(2, 4, 4, 4, 8, w[1]).transpose(1, 0, 2, 3, 4, 5)
    c = c.reshape(2, 4, 4, 4, 8, w[2]).transpose(2, 0, 3, 1, 4, 5)
    return jnp.concatenate([a, b, c], axis=-1).reshape(1024, 2048)


def per_device(tokens, routes, route_weights, cotangent, gate_weight, up_weight, down_weight):
    out = dispatch(tokens, cotangent, routes, route_weights)
    slot_rows, slot_cots = canonical(out[0:3]), canonical(out[3:6])
    extra = out[6].reshape(2, 4, 4, 4, 8, 128).transpose(3, 0, 1, 2, 4, 5).reshape(1024, 128).astype(jnp.float32)
    own = lax.axis_index(("node", "rail")) + 1
    weight = jnp.sum(
        jnp.where(extra[:, :8] == own.astype(jnp.float32), extra[:, 8:16] + extra[:, 16:24] + extra[:, 24:32], 0.0), axis=1
    )
    slot_grads = (weight[:, None] * slot_cots.astype(jnp.float32)).astype(jnp.bfloat16)
    token_count, model_width = tokens.shape
    top_count = routes.shape[1]
    experts, capacity = 128, 8
    flat_routes = routes.reshape(-1)
    onehot = (flat_routes[:, None] == jnp.arange(experts, dtype=jnp.int32)[None, :]).astype(jnp.int32)
    position = jnp.sum((jnp.cumsum(onehot, axis=0) - onehot) * onehot, axis=1)
    slot_index = flat_routes * capacity + position
    w_gate, w_up, w_down = gate_weight[0], up_weight[0], down_weight[0]
    gate_pre, up_pre, hidden, output = expert_forward(slot_rows, w_gate, w_up, w_down)
    names = ("node", "rail")
    out_home = lax.all_to_all(
        output.reshape(experts, capacity, model_width), names, split_axis=0, concat_axis=0, tiled=True
    )
    input_back, gate_grad, up_grad, down_grad = expert_backward(
        slot_rows, slot_grads, gate_pre, up_pre, hidden, w_gate, w_up, w_down
    )
    back_home = lax.all_to_all(
        input_back.reshape(experts, capacity, model_width), names, split_axis=0, concat_axis=0, tiled=True
    )
    out_slot = out_home.reshape(-1, model_width)[slot_index].reshape(token_count, top_count, model_width)
    back_slot = back_home.reshape(-1, model_width)[slot_index].reshape(token_count, top_count, model_width)
    mixed, token_grad, weight_grad = combine_slots(out_slot, back_slot, route_weights, cotangent)
    return (mixed, token_grad, weight_grad, gate_grad[None], up_grad[None], down_grad[None])


def solution(mesh):
    placed = (
        P(("node", "rail"), None),
        P(("node", "rail"), None),
        P(("node", "rail"), None),
        P(("node", "rail"), None),
        P(("node", "rail"), None, None),
        P(("node", "rail"), None, None),
        P(("node", "rail"), None, None),
    )
    return jax.shard_map(
        per_device,
        mesh=mesh,
        in_specs=placed,
        out_specs=(
            P(("node", "rail"), None),
            P(("node", "rail"), None),
            P(("node", "rail"), None),
            P(("node", "rail"), None, None),
            P(("node", "rail"), None, None),
            P(("node", "rail"), None, None),
        ),
        check_vma=False,
    )
```

```python
import jax
import jax.numpy as jnp
from jax import lax
from jax.experimental import pallas as pl
from jax.experimental.pallas import tpu as pltpu
from jax.sharding import PartitionSpec as P

MESH = pl.DeviceIdType.MESH
F32, BF16 = jnp.float32, jnp.bfloat16
PARTS = ((0, 1, 2, 0, 768), (1, 2, 0, 768, 640), (2, 0, 1, 1408, 640))


def place():
    node, rail = lax.axis_index("node"), lax.axis_index("rail")
    return (node // 2, rail % 4, rail // 4), node % 2


def moved(co, axis, value):
    return tuple(value if i == axis else v for i, v in enumerate(co))


def device(co, core):
    return (co[0] * 2 + core, co[2] * 4 + co[1])


def remote(src, dst, send, recv, target):
    return pltpu.make_async_remote_copy(
        src_ref=src, dst_ref=dst, send_sem=send, recv_sem=recv, device_id=target, device_id_type=MESH
    )


def greet(co, core):
    barrier = pltpu.get_barrier_semaphore()
    targets = [device(co, 1 - core)]
    for axis in range(3):
        for step in (1, 2, 3):
            there = moved(co, axis, (co[axis] + step) % 4)
            targets += [device(there, core), device(there, 1 - core)]
    for target in targets:
        pl.semaphore_signal(barrier, inc=1, device_id=target, device_id_type=MESH)
    return barrier, len(targets)


def route_tables(routes, weights):
    lanes = lax.broadcasted_iota(jnp.int32, (64, 128), 1)
    named = jnp.zeros((64, 128), F32)
    for k in range(8):
        named = named + jnp.where(routes[:, k : k + 1] == lanes, 1.0, 0.0)
    row = lax.broadcasted_iota(jnp.int32, (64, 64), 0)
    col = lax.broadcasted_iota(jnp.int32, (64, 64), 1)
    upto = jnp.where(col <= row, 1.0, 0.0).astype(BF16)
    counted = jnp.dot(upto, named.astype(BF16), preferred_element_type=F32)
    table = (counted * named).astype(BF16)
    extra = jnp.zeros((64, 128), F32)
    for k in range(8):
        w = weights[:, k : k + 1]
        high = w.astype(BF16).astype(F32)
        mid = (w - high).astype(BF16).astype(F32)
        low = w - high - mid
        extra = jnp.where(lanes == k, (routes[:, k : k + 1] + 1).astype(F32), extra)
        extra = jnp.where(lanes == 8 + k, high, extra)
        extra = jnp.where(lanes == 16 + k, mid, extra)
        extra = jnp.where(lanes == 24 + k, low, extra)
    return table, extra.astype(BF16)


def one_hot(table, co, slot_axis):
    expert = lax.broadcasted_iota(jnp.int32, (128, 256), 0)
    lane = lax.broadcasted_iota(jnp.int32, (128, 256), 1)
    core, along = lane // 128, (lane // 32) % 4
    there = moved(co, slot_axis, along)
    owner = (there[0] * 2 + core) * 16 + there[2] * 4 + there[1]
    spread = jnp.dot(table, jnp.where(expert == owner, 1.0, 0.0).astype(BF16), preferred_element_type=F32)
    row = lax.broadcasted_iota(jnp.int32, (256, 256), 0)
    lane = lax.broadcasted_iota(jnp.int32, (256, 256), 1)
    wanted = jnp.where(row // 64 == (lane // 8) % 4, lane % 8 + 1, -1).astype(F32)
    return jnp.where(spread == wanted, 1.0, 0.0).astype(BF16)


def dispatch_kernel(tok, cot, routes, weights, *refs):
    xo, co_, rwo, st = refs[0:3], refs[3:6], refs[6], refs[7]
    xb, cb, qb, rwb = refs[8:11], refs[11:14], refs[14:17], refs[17]
    xs, cs, rws = refs[18:21], refs[21:24], refs[24]
    s1, r1, s2, r2, s3, r3, loc = refs[25:32]
    co, core = place()
    barrier, count = greet(co, core)
    table, extra = route_tables(routes[...], weights[...])
    for p, (a1, a2, _, c0, cols) in enumerate(PARTS):
        xb[p][co[a2], co[a1]] = tok[:, c0 : c0 + cols]
        cb[p][co[a2], co[a1]] = cot[:, c0 : c0 + cols]
        qb[p][co[a2], co[a1]] = table
    rwb[co[1], co[0]] = extra
    pl.semaphore_wait(barrier, count)

    tables = [(qb[p], p, p) for p in range(3)] + [(rwb, 0, 3)]
    rows = [(xb[p], p, 4 + p) for p in range(3)]
    grads = [(cb[p], p, 7 + p) for p in range(3)]

    def first_copies(buf, p, n):
        a1, a2 = PARTS[p][:2]
        mine = buf.at[co[a2], co[a1]]
        return [
            remote(mine, mine, s1.at[n, d - 1], r1.at[n, co[a1]], device(moved(co, a1, (co[a1] + d) % 4), core))
            for d in (1, 2, 3)
        ]

    def first_wait(buf, p, n):
        a1, a2 = PARTS[p][:2]
        for d in (1, 2, 3):
            i = (co[a1] + d) % 4
            got = buf.at[co[a2], i]
            remote(got, got, s1.at[n, d - 1], r1.at[n, i], device(moved(co, a1, i), core)).wait_recv()

    def half(buf, block, h):
        return buf.at[block, pl.ds(2 * h, 2)]

    def second_copy(buf, p, n, block, h, right, number):
        a2 = PARTS[p][1]
        part = half(buf, block, h)
        target = device(moved(co, a2, (co[a2] + (1 if right else 3)) % 4), core)
        return remote(part, part, s2.at[n, number], r2.at[n, block, h], target)

    def second_first(buf, p, n):
        me = co[PARTS[p][1]]
        return [
            second_copy(buf, p, n, me, 0, True, 0),
            second_copy(buf, p, n, me, 1, False, 1),
            second_copy(buf, p, n, me, 1, True, 2),
            second_copy(buf, p, n, me, 0, False, 3),
        ]

    def second_wait(buf, p, n, d, h):
        a2 = PARTS[p][1]
        block = (co[a2] + d) % 4
        second_copy(buf, p, n, block, h, True, 0).wait_recv()

    def relay(buf, p, n):
        a2 = PARTS[p][1]
        second_wait(buf, p, n, 3, 0)
        a = second_copy(buf, p, n, (co[a2] + 3) % 4, 0, True, 4)
        a.start()
        second_wait(buf, p, n, 1, 1)
        b = second_copy(buf, p, n, (co[a2] + 1) % 4, 1, False, 5)
        b.start()
        return [a, b]

    def rest_wait(buf, p, n):
        second_wait(buf, p, n, 3, 1)
        second_wait(buf, p, n, 1, 0)
        second_wait(buf, p, n, 2, 0)
        second_wait(buf, p, n, 2, 1)

    sent = []

    def start(copies):
        for c in copies:
            c.start()
        sent.extend(copies)

    for item in tables + rows + grads:
        start(first_copies(*item))
    for item in tables + rows:
        first_wait(*item)
        start(second_first(*item))
    for item in grads:
        first_wait(*item)
        start(second_first(*item))
    for item in tables + rows:
        sent.extend(relay(*item))
    for item in tables:
        rest_wait(*item)
    for p, (_, _, slot_axis, _, _) in enumerate(PARTS):

        def build(g, _, p=p, slot_axis=slot_axis):
            st[p, g] = one_hot(qb[p][g].reshape(256, 128), co, slot_axis)
            return 0

        lax.fori_loop(0, 4, build, 0)

    def pick(buf, out, p):
        cols = buf.shape[-1]

        def step(g, _):
            r = lax.dot_general(
                st[p, g], buf[g].reshape(256, cols), (((0,), (0,)), ((), ())), preferred_element_type=F32
            )
            out[:, pl.ds(pl.multiple_of(g * 32, 32), 32), :] = r.astype(BF16).reshape(8, 32, cols)
            return 0

        lax.fori_loop(0, 4, step, 0)

    def slot_copies(src, dst, p, n):
        axis = PARTS[p][2]
        me = core * 4 + co[axis]
        remotes = []
        for dc in (0, 1):
            for d in (1, 3, 2, 0):
                if dc == 0 and d == 0:
                    continue
                there, other = (co[axis] + d) % 4, (core + dc) % 2
                k = other * 4 + there
                remotes.append(
                    remote(src.at[k], dst.at[me], s3.at[n, dc * 4 + d], r3.at[n, me], device(moved(co, axis, there), other))
                )
        return remotes, pltpu.make_async_copy(src.at[me], dst.at[me], loc.at[n])

    def slot_wait(src, dst, p, n):
        axis = PARTS[p][2]
        for dc in (0, 1):
            for d in (1, 3, 2, 0):
                if dc == 0 and d == 0:
                    continue
                there, other = (co[axis] + d) % 4, (core + dc) % 2
                k = other * 4 + there
                remote(src.at[k], dst.at[k], s3.at[n, dc * 4 + d], r3.at[n, k], device(moved(co, axis, there), other)).wait_recv()

    slots = []

    def send(src, dst, p, n):
        remotes, local = slot_copies(src, dst, p, n)
        start(remotes)
        local.start()
        slots.append((src, dst, p, n, local))

    pick(rwb, rws, 0)
    send(rws, rwo, 0, 0)
    for p in range(3):
        rest_wait(*rows[p])
        pick(xb[p], xs[p], p)
        send(xs[p], xo[p], p, 1 + p)
    for item in grads:
        sent.extend(relay(*item))
    for p in range(3):
        rest_wait(*grads[p])
        pick(cb[p], cs[p], p)
        send(cs[p], co_[p], p, 4 + p)
    for src, dst, p, n, local in slots:
        slot_wait(src, dst, p, n)
        local.wait()
    for c in sent:
        c.wait_send()


def dispatch(tokens, cotangent, routes, weights):
    widths = [part[4] for part in PARTS]
    outs = (
        [jax.ShapeDtypeStruct((8, 128, w), BF16) for w in widths] * 2
        + [jax.ShapeDtypeStruct((8, 128, 128), BF16), jax.ShapeDtypeStruct((3, 4, 256, 256), BF16)]
    )
    any_, vmem = pl.BlockSpec(memory_space=pl.ANY), pl.BlockSpec(memory_space=pltpu.VMEM)
    gathered = [pltpu.VMEM((4, 4, 64, w), BF16) for w in widths]
    table = pltpu.VMEM((4, 4, 64, 128), BF16)
    sends = [pltpu.VMEM((8, 128, w), BF16) for w in widths]
    dma = pltpu.SemaphoreType.DMA
    return pl.pallas_call(
        dispatch_kernel,
        out_shape=outs,
        in_specs=[vmem] * 4,
        out_specs=[any_] * 7 + [vmem],
        scratch_shapes=gathered * 2 + [table] * 4 + sends * 2 + [pltpu.VMEM((8, 128, 128), BF16)]
        + [dma((10, 3)), dma((10, 4)), dma((10, 6)), dma((10, 4, 2)), dma((7, 8)), dma((7, 8)), dma((7,))],
        compiler_params=pltpu.CompilerParams(
            collective_id=0, has_side_effects=True, vmem_limit_bytes=56 * 2**20
        ),
    )(tokens, cotangent, routes, weights)


def pieces(p):
    for k in range(8):
        c, d = k // 4, k % 4
        if p == 0:
            yield k * 128, 128, (k,)
        elif p == 1:
            yield k * 128, 128, (slice(4 * c, 4 * c + 4), slice(None), d)
        else:
            for x in range(4):
                yield k * 128 + x * 32, 32, (slice(4 * c, 4 * c + 4), d, x)


def tiles(cols, body):
    def step(n, _):
        body(pl.multiple_of(n * 256, 256), 256)
        return 0

    lax.fori_loop(0, cols // 256, step, 0)
    if cols % 256:
        body(cols - cols % 256, cols % 256)


def contract(a, b, da, db):
    return lax.dot_general(a, b, (((da,), (db,)), ((), ())), preferred_element_type=F32)


def expert_kernel(xi, xi1, xi2, ci, ci1, ci2, rwi, sti, wgi, wui, wdi, *refs):
    mixed, tgrad, vgrad, ggrad, ugrad, dgrad = refs[0:6]
    back_in = refs[6:13]
    refs = refs[13:]
    x, c, rw, st = refs[0:3], refs[3:6], refs[6], refs[7]
    wg, wu, wd = refs[8:11]
    ag, au, ah = refs[11:14]
    hw, gb, ub = refs[14:17], refs[17], refs[18]
    send = refs[19:26]
    ring = refs[26:33]
    line = refs[33:40]
    wcol, rep, stage = refs[40:43]
    ld, s4, r4, loc, s5, r5, s6, r6, sg = refs[43:52]
    co, core = place()
    loads = [
        pltpu.make_async_copy(src, dst, ld.at[i])
        for i, (src, dst) in enumerate(
            zip((xi, xi1, xi2, rwi, wgi, wui, wdi, ci, ci1, ci2, sti), (*x, rw, wg, wu, wd, *c, st), strict=True)
        )
    ]
    for load in loads:
        load.start()
    barrier, count = greet(co, core)
    own = ((co[0] * 2 + core) * 16 + co[2] * 4 + co[1] + 1).astype(F32)
    widths = [part[4] for part in PARTS]

    for load in loads[:6]:
        load.wait()

    def pre(n, _):
        n0 = pl.multiple_of(n * 256, 256)
        for w, acc in ((wg, ag), (wu, au)):
            for p, (_, _, _, c0, cols) in enumerate(PARTS):
                r = jnp.dot(
                    x[p][...].reshape(1024, cols), w[c0 : c0 + cols, pl.ds(n0, 256)], preferred_element_type=F32
                )
                for row, rows, at in pieces(p):
                    piece = r[row : row + rows]
                    at = (*at, *([slice(None)] * (4 - len(at))), pl.ds(n0, 256))
                    where = acc.at[at]
                    piece = piece.reshape(where.shape)
                    where[...] = piece if p == 0 else where[...] + piece
        return 0

    lax.fori_loop(0, 3, pre, 0)

    lane = lax.broadcasted_iota(jnp.int32, (128, 128), 1)
    row = lax.broadcasted_iota(jnp.int32, (128, 128), 0)
    spread = jnp.where((row < 8) & (lane < 32) & (lane % 8 == row), 1.0, 0.0).astype(BF16)

    def weigh(k, _):
        route = jnp.dot(rw[k], spread, preferred_element_type=F32)
        taken = jnp.where((route == own) & (lane >= 8), rw[k].astype(F32), 0.0)
        wcol[k] = jnp.broadcast_to(jnp.sum(taken, axis=1, keepdims=True), (128, 128))
        rep[k] = route
        return 0

    lax.fori_loop(0, 8, weigh, 0)

    def activate(i, _):
        k, y = i // 4, i % 4
        rows = pl.ds(pl.multiple_of(y * 32, 32), 32)
        g, u = ag[k, y].reshape(32, 768), au[k, y].reshape(32, 768)
        w = wcol[k, rows, 0:1]
        ah[k, y] = (g * jax.nn.sigmoid(g) * u * w).reshape(4, 8, 768)
        return 0

    lax.fori_loop(0, 32, activate, 0)

    def ordered(acc, out, p):
        for row, rows, at in pieces(p):
            out[row : row + rows, :] = acc[at].reshape(rows, 768).astype(BF16)

    for p in range(3):
        ordered(ah, hw[p], p)
    pl.semaphore_wait(barrier, count)
    loads[6].wait()

    sent = []

    def slot_ends(p):
        axis = PARTS[p][2]
        for dc in (0, 1):
            for d in (1, 3, 2, 0):
                if dc == 0 and d == 0:
                    continue
                there, other = (co[axis] + d) % 4, (core + dc) % 2
                yield dc * 4 + d, other * 4 + there, device(moved(co, axis, there), other)

    slot_sent = {}

    def slot_start(p, n):
        me = core * 4 + co[PARTS[p][2]]
        src, dst = send[n], back_in[n]
        copies = [remote(src.at[k], dst.at[me], s4.at[n, i], r4.at[n, me], to) for i, k, to in slot_ends(p)]
        for copy in copies:
            copy.start()
        local = pltpu.make_async_copy(src.at[me], dst.at[me], loc.at[n])
        local.start()
        slot_sent[n] = (copies, local)

    def slot_finish(p, n):
        copies, local = slot_sent[n]
        local.wait()
        for copy in copies:
            copy.wait_send()
        for i, k, to in slot_ends(p):
            remote(send[n].at[k], back_in[n].at[k], s4.at[n, i], r4.at[n, k], to).wait_recv()

    for p, (_, _, _, c0, cols) in enumerate(PARTS):

        def forward(n0, width, p=p, c0=c0):
            r = jnp.dot(hw[p][...], wd[:, pl.ds(c0 + n0, width)], preferred_element_type=F32)
            send[p][:, :, pl.ds(n0, width)] = r.astype(BF16).reshape(8, 128, width)

        tiles(cols, forward)
        slot_start(p, p)

    for load in loads[7:]:
        load.wait()

    def hidden_back(n, _):
        n0 = pl.multiple_of(n * 256, 256)
        for p, (_, _, _, c0, cols) in enumerate(PARTS):
            r = contract(c[p][...].reshape(1024, cols), wd[pl.ds(n0, 256), c0 : c0 + cols], 1, 1)
            for row, rows, at in pieces(p):
                piece = r[row : row + rows]
                at = (*at, *([slice(None)] * (4 - len(at))), pl.ds(n0, 256))
                where = ah.at[at]
                piece = piece.reshape(where.shape)
                where[...] = piece if p == 0 else where[...] + piece
        return 0

    lax.fori_loop(0, 3, hidden_back, 0)
    lane32 = lax.broadcasted_iota(jnp.int32, (32, 128), 1)

    def derive(i, _):
        k, y = i // 4, i % 4
        rows = pl.ds(pl.multiple_of(y * 32, 32), 32)
        g, u, h = ag[k, y].reshape(32, 768), au[k, y].reshape(32, 768), ah[k, y].reshape(32, 768)
        w = wcol[k, rows, 0:1]
        s = jax.nn.sigmoid(g)
        silu = g * s
        value = jnp.sum(silu * u * h, axis=1, keepdims=True)
        high = value.astype(BF16).astype(F32)
        match = rep[k, rows] == own
        both = jnp.where(lane32 < 8, high, jnp.where(lane32 < 16, value - high, 0.0))
        send[6][k, rows] = jnp.where(match, both, 0.0).astype(BF16)
        h = h * w
        ag[k, y] = (h * u * s * (1.0 + g * (1.0 - s))).reshape(4, 8, 768)
        au[k, y] = (h * silu).reshape(4, 8, 768)
        return 0

    lax.fori_loop(0, 32, derive, 0)
    slot_start(0, 6)
    for p, (_, _, _, c0, cols) in enumerate(PARTS):
        ordered(ag, gb, p)
        ordered(au, ub, p)

        def backward(n0, width, p=p, c0=c0):
            rows = pl.ds(c0 + n0, width)
            r = contract(gb[...], wg[rows, :], 1, 1) + contract(ub[...], wu[rows, :], 1, 1)
            send[3 + p][:, :, pl.ds(n0, width)] = r.astype(BF16).reshape(8, 128, width)

        tiles(cols, backward)
        slot_start(p, 3 + p)

    def neighbour(p, d):
        a2 = PARTS[p][1]
        return device(moved(co, a2, (co[a2] + d) % 4), core)

    def ring_copy(p, n, chunk, kind):
        to_right = kind in (0, 2, 3)
        return remote(send[n].at[chunk], ring[n].at[kind], s5.at[n, kind], r5.at[n, kind], neighbour(p, 1 if to_right else 3))

    def go(copy):
        copy.start()
        sent.append(copy)

    def ring_first(p, n):
        slot_finish(p, n)
        cols = send[n].shape[-1]
        me = co[PARTS[p][1]]
        for d in (2, 1, 3, 0):
            g = (me + d) % 4
            copy = pltpu.make_async_copy(
                back_in[n].at[:, pl.ds(pl.multiple_of(g * 32, 32), 32)], stage.at[:, :, pl.ds(0, cols)], loc.at[n]
            )
            copy.start()
            copy.wait()
            r = jnp.dot(st[p, g], stage[:, :, 0:cols].reshape(256, cols), preferred_element_type=F32)
            send[n][pl.ds(2 * g, 2)] = r.astype(BF16).reshape(2, 128, cols)
            if d == 2:
                go(ring_copy(p, n, 2 * g, 0))
                go(ring_copy(p, n, 2 * g + 1, 1))
            if d == 1:
                go(ring_copy(p, n, 2 * g + 1, 3))
            if d == 3:
                go(ring_copy(p, n, 2 * g, 4))

    def ring_pass(p, n):
        me = co[PARTS[p][1]]
        for kind, chunk, out in ((0, 2 * ((me + 1) % 4), 2), (1, 2 * ((me + 3) % 4) + 1, 5)):
            ring_copy(p, n, chunk, kind).wait_recv()
            send[n][chunk] = (send[n][chunk].astype(F32) + ring[n][kind].astype(F32)).astype(BF16)
            go(ring_copy(p, n, chunk, out))

    def line_copy(p, n, i, d):
        a1, a2 = PARTS[p][:2]
        rows = pl.ds(pl.multiple_of((i % 2) * 64, 64), 64)
        return rows, remote(
            send[n].at[2 * co[a2] + i // 2, rows],
            line[n].at[co[a1]],
            s6.at[n, d - 1],
            r6.at[n, co[a1]],
            device(moved(co, a1, (co[a1] + d) % 4), core),
        )

    def line_first(p, n):
        a1, a2 = PARTS[p][:2]
        for h in (0, 1):
            chunk = 2 * co[a2] + h
            ring_copy(p, n, chunk, 2 + h).wait_recv()
            ring_copy(p, n, chunk, 4 + h).wait_recv()
            total = send[n][chunk].astype(F32) + ring[n][2 + h].astype(F32) + ring[n][4 + h].astype(F32)
            send[n][chunk] = total.astype(BF16)
        for d in (2, 1, 3):
            go(line_copy(p, n, (co[a1] + d) % 4, d)[1])

    def line_last(p, n):
        a1, a2 = PARTS[p][:2]
        i = co[a1]
        rows = pl.ds(pl.multiple_of((i % 2) * 64, 64), 64)
        total = send[n][2 * co[a2] + i // 2, rows].astype(F32)
        for d in (1, 2, 3):
            j = (i + d) % 4
            got = line[n].at[j]
            remote(got, got, s6.at[n, d - 1], r6.at[n, j], device(moved(co, a1, j), core)).wait_recv()
            total = total + line[n][j].astype(F32)
        return total

    outs = [(p, p) for p in range(3)]
    backs = [(0, 6)] + [(p, 3 + p) for p in range(3)]
    for item in outs:
        ring_first(*item)
    for p, (_, _, _, c0, cols) in enumerate(PARTS):

        def down(n, _, p=p, c0=c0, cols=cols):
            n0 = pl.ds(pl.multiple_of(n * 256, 256), 256)
            wd[n0, c0 : c0 + cols] = contract(hw[p][:, n0], c[p][...].reshape(1024, cols), 0, 0).astype(BF16)
            return 0

        lax.fori_loop(0, 3, down, 0)
    grads = [pltpu.make_async_copy(wd, dgrad, sg.at[0])]
    grads[0].start()
    for item in outs:
        ring_pass(*item)
    for item in backs:
        ring_first(*item)
    for item in outs:
        line_first(*item)

    def rows_of(p):
        c0, cols = PARTS[p][3:]

        def gate(n0, width):
            part = x[p][:, :, pl.ds(n0, width)].reshape(1024, width)
            rows = pl.ds(c0 + n0, width)
            wg[rows, :] = contract(part, gb[...], 0, 0).astype(BF16)
            wu[rows, :] = contract(part, ub[...], 0, 0).astype(BF16)

        tiles(cols, gate)
        for i, (src, dst) in enumerate(((wg, ggrad), (wu, ugrad))):
            copy = pltpu.make_async_copy(src.at[pl.ds(c0, cols)], dst.at[pl.ds(c0, cols)], sg.at[1 + 2 * p + i])
            copy.start()
            grads.append(copy)

    rows_of(2)
    for item in backs:
        ring_pass(*item)
    ordered(ag, gb, 1)
    ordered(au, ub, 1)
    rows_of(1)
    for item in backs:
        line_first(*item)
    ordered(ag, gb, 0)
    ordered(au, ub, 0)
    rows_of(0)
    for p, (_, _, _, c0, cols) in enumerate(PARTS):
        mixed[:, c0 : c0 + cols] = line_last(p, p).astype(BF16)
        tgrad[:, c0 : c0 + cols] = line_last(p, 3 + p).astype(BF16)
    vgrad[...] = line_last(0, 6)
    for copy in sent:
        copy.wait_send()
    for copy in grads:
        copy.wait()


def expert(out, gate_weight, up_weight, down_weight):
    widths = [part[4] for part in PARTS]
    shape = jax.ShapeDtypeStruct
    any_, vmem = pl.BlockSpec(memory_space=pl.ANY), pl.BlockSpec(memory_space=pltpu.VMEM)
    items = widths * 2 + [128]
    outs = [
        shape((64, 2048), BF16),
        shape((64, 2048), BF16),
        shape((64, 128), F32),
        shape((2048, 768), BF16),
        shape((2048, 768), BF16),
        shape((768, 2048), BF16),
    ] + [shape((8, 128, w), BF16) for w in items]
    slots = [pltpu.VMEM((8, 128, w), BF16) for w in widths]
    dma = pltpu.SemaphoreType.DMA
    got = pl.pallas_call(
        expert_kernel,
        out_shape=outs,
        in_specs=[any_] * 11,
        out_specs=[vmem] * 3 + [any_] * 10,
        scratch_shapes=slots * 2
        + [pltpu.VMEM((8, 128, 128), BF16), pltpu.VMEM((3, 4, 256, 256), BF16)]
        + [pltpu.VMEM((2048, 768), BF16)] * 2
        + [pltpu.VMEM((768, 2048), BF16)]
        + [pltpu.VMEM((8, 4, 4, 8, 768), F32)] * 3
        + [pltpu.VMEM((1024, 768), BF16)] * 5
        + [pltpu.VMEM((8, 128, w), BF16) for w in items]
        + [pltpu.VMEM((6, 128, w), BF16) for w in items]
        + [pltpu.VMEM((4, 64, w), BF16) for w in items]
        + [pltpu.VMEM((8, 128, 128), F32)] * 2
        + [pltpu.VMEM((8, 32, 768), BF16)]
        + [dma((11,)), dma((7, 8)), dma((7, 8)), dma((7,)), dma((7, 6)), dma((7, 6)), dma((7, 3)), dma((7, 4)), dma((7,))],
        compiler_params=pltpu.CompilerParams(
            collective_id=1, has_side_effects=True, vmem_limit_bytes=62 * 2**20
        ),
    )(*out, gate_weight, up_weight, down_weight)
    return got[:6]


def per_device(tokens, routes, route_weights, cotangent, gate_weight, up_weight, down_weight):
    out = dispatch(tokens, cotangent, routes, route_weights)
    mixed, token_grad, value, gate_grad, up_grad, down_grad = expert(out, gate_weight[0], up_weight[0], down_weight[0])
    weight_grad = value[:, 0:8] + value[:, 8:16]
    return (mixed, token_grad, weight_grad, gate_grad[None], up_grad[None], down_grad[None])


def solution(mesh):
    placed = (
        P(("node", "rail"), None),
        P(("node", "rail"), None),
        P(("node", "rail"), None),
        P(("node", "rail"), None),
        P(("node", "rail"), None, None),
        P(("node", "rail"), None, None),
        P(("node", "rail"), None, None),
    )
    return jax.shard_map(
        per_device,
        mesh=mesh,
        in_specs=placed,
        out_specs=(
            P(("node", "rail"), None),
            P(("node", "rail"), None),
            P(("node", "rail"), None),
            P(("node", "rail"), None, None),
            P(("node", "rail"), None, None),
            P(("node", "rail"), None, None),
        ),
        check_vma=False,
    )
```

```python
import jax
import jax.numpy as jnp
from jax import lax
from jax.experimental import pallas as pl
from jax.experimental.pallas import tpu as pltpu
from jax.sharding import PartitionSpec as P

MESH = pl.DeviceIdType.MESH
F32, BF16 = jnp.float32, jnp.bfloat16
PARTS = ((0, 1, 2, 0, 768), (1, 2, 0, 768, 640), (2, 0, 1, 1408, 640))


def place():
    node, rail = lax.axis_index("node"), lax.axis_index("rail")
    return (node // 2, rail % 4, rail // 4), node % 2


def moved(co, axis, value):
    return tuple(value if i == axis else v for i, v in enumerate(co))


def device(co, core):
    return (co[0] * 2 + core, co[2] * 4 + co[1])


def remote(src, dst, send, recv, target):
    return pltpu.make_async_remote_copy(
        src_ref=src, dst_ref=dst, send_sem=send, recv_sem=recv, device_id=target, device_id_type=MESH
    )


def greet(co, core):
    barrier = pltpu.get_barrier_semaphore()
    targets = [device(co, 1 - core)]
    for axis in range(3):
        for step in (1, 2, 3):
            there = moved(co, axis, (co[axis] + step) % 4)
            targets += [device(there, core), device(there, 1 - core)]
    for target in targets:
        pl.semaphore_signal(barrier, inc=1, device_id=target, device_id_type=MESH)
    return barrier, len(targets)


def one_hot(table, co, slot_axis):
    expert = lax.broadcasted_iota(jnp.int32, (128, 256), 0)
    lane = lax.broadcasted_iota(jnp.int32, (128, 256), 1)
    core, along = lane // 128, (lane // 32) % 4
    there = moved(co, slot_axis, along)
    owner = (there[0] * 2 + core) * 16 + there[2] * 4 + there[1]
    spread = jnp.dot(table, jnp.where(expert == owner, 1.0, 0.0).astype(BF16), preferred_element_type=F32)
    row = lax.broadcasted_iota(jnp.int32, (256, 256), 0)
    lane = lax.broadcasted_iota(jnp.int32, (256, 256), 1)
    wanted = jnp.where(row // 64 == (lane // 8) % 4, lane % 8 + 1, -1).astype(F32)
    return jnp.where(spread == wanted, 1.0, 0.0).astype(BF16)


def pieces(p):
    for k in range(8):
        c, d = k // 4, k % 4
        if p == 0:
            yield k * 128, 128, (k,)
        elif p == 1:
            yield k * 128, 128, (slice(4 * c, 4 * c + 4), slice(None), d)
        else:
            for x in range(4):
                yield k * 128 + x * 32, 32, (slice(4 * c, 4 * c + 4), d, x)


def tiles(cols, body):
    def step(n, _):
        body(pl.multiple_of(n * 256, 256), 256)
        return 0

    lax.fori_loop(0, cols // 256, step, 0)
    if cols % 256:
        body(cols - cols % 256, cols % 256)


def contract(a, b, da, db):
    return lax.dot_general(a, b, (((da,), (db,)), ((), ())), preferred_element_type=F32)


def route_tables(routes, weights):
    lanes = lax.broadcasted_iota(jnp.int32, (64, 128), 1).astype(F32)
    ids = routes.astype(F32).astype(BF16)
    rows8 = lax.broadcasted_iota(jnp.int32, (8, 128), 0)
    named = jnp.zeros((64, 128), F32)
    for k in range(8):
        pick = jnp.where(rows8 == k, 1.0, 0.0).astype(BF16)
        named = named + jnp.where(contract(ids, pick, 0, 0) == lanes, 1.0, 0.0)
    row = lax.broadcasted_iota(jnp.int32, (64, 64), 0)
    col = lax.broadcasted_iota(jnp.int32, (64, 64), 1)
    upto = jnp.where(col <= row, 1.0, 0.0).astype(BF16)
    counted = jnp.dot(upto, named.astype(BF16), preferred_element_type=F32)
    table = (counted * named).astype(BF16)
    high = weights.astype(BF16)
    mid = (weights - high.astype(F32)).astype(BF16)
    low = (weights - high.astype(F32) - mid.astype(F32)).astype(BF16)
    lane8 = lax.broadcasted_iota(jnp.int32, (8, 128), 1)
    extra = jnp.zeros((64, 128), F32)
    for i, part in enumerate(((routes + 1).astype(F32).astype(BF16), high, mid, low)):
        extra = extra + contract(part, jnp.where(lane8 == rows8 + 8 * i, 1.0, 0.0).astype(BF16), 0, 0)
    return table, extra.astype(BF16)


def moe_kernel(tok, cot, routes, weights, wgi, wui, wdi, *refs):
    ggrad, ugrad, dgrad = refs[0:3]
    ring, line = refs[3:10], refs[10:17]
    refs = refs[17:]
    xb, cb, vr, qb, rwb = refs[0:3], refs[3:6], refs[6], refs[7:10], refs[10]
    send = refs[11:18]
    x, c, rw, st = refs[18:21], refs[21:24], refs[24], refs[25]
    wg, wu, wd = refs[26:29]
    ag, au, ah = refs[29:32]
    hw, gb, ub, wcol = refs[32:35], refs[35], refs[36], refs[37]
    s1, r1, s2, r2, s3, r3, loc3, ld, s4, r4, loc4, s5, r5, s6, r6, sg, ls = refs[38:55]
    co, core = place()
    own = ((co[0] * 2 + core) * 16 + co[2] * 4 + co[1] + 1).astype(F32)
    barrier, count = greet(co, core)
    loads = [pltpu.make_async_copy(src, dst, ld.at[i]) for i, (src, dst) in enumerate(((wgi, wg), (wui, wu), (wdi, wd)))]

    def half_rows(i):
        return pl.ds(pl.multiple_of((i % 2) * 64, 64), 64)

    def source(p, i2, i1):
        return 2 * i2 + i1 // 2, half_rows(i1)

    rows = [(xb[p], p, p) for p in range(3)]
    grads = [(cb[p], p, 3 + p) for p in range(3)]
    tables = [(qb[p], p, 6 + p) for p in range(3)] + [(rwb, 0, 9)]

    def put(buf, p, value):
        a1, a2 = PARTS[p][:2]
        chunk, at = source(p, co[a2], co[a1])
        buf[chunk, at] = value

    flying = {}

    def launch(n, copies):
        for copy in copies:
            copy.start()
        flying.setdefault(n, []).extend(copies)

    def landed(n):
        for copy in flying.pop(n):
            copy.wait_send()

    def first_start(buf, p, n):
        a1, a2 = PARTS[p][:2]
        chunk, at = source(p, co[a2], co[a1])
        mine = buf.at[chunk, at]
        launch(n, [
            remote(mine, mine, s1.at[n, d - 1], r1.at[n, co[a1]], device(moved(co, a1, (co[a1] + d) % 4), core))
            for d in (2, 1, 3)
        ])

    def first_wait(buf, p, n):
        a1, a2 = PARTS[p][:2]
        for d in (1, 2, 3):
            i = (co[a1] + d) % 4
            chunk, at = source(p, co[a2], i)
            got = buf.at[chunk, at]
            remote(got, got, s1.at[n, d - 1], r1.at[n, i], device(moved(co, a1, i), core)).wait_recv()

    def second_copy(buf, p, n, block, h, right, number):
        a2 = PARTS[p][1]
        part = buf.at[2 * block + h]
        target = device(moved(co, a2, (co[a2] + (1 if right else 3)) % 4), core)
        return remote(part, part, s2.at[n, number], r2.at[n, block, h], target)

    def second_start(buf, p, n):
        me = co[PARTS[p][1]]
        launch(n, [
            second_copy(buf, p, n, me, 0, True, 0),
            second_copy(buf, p, n, me, 1, False, 1),
            second_copy(buf, p, n, me, 1, True, 2),
            second_copy(buf, p, n, me, 0, False, 3),
        ])

    def second_wait(buf, p, n, d, h):
        second_copy(buf, p, n, (co[PARTS[p][1]] + d) % 4, h, True, 0).wait_recv()

    def relay(buf, p, n):
        me = co[PARTS[p][1]]
        second_wait(buf, p, n, 3, 0)
        launch(n, [second_copy(buf, p, n, (me + 3) % 4, 0, True, 4)])
        second_wait(buf, p, n, 1, 1)
        launch(n, [second_copy(buf, p, n, (me + 1) % 4, 1, False, 5)])

    def rest_wait(buf, p, n):
        for d, h in ((3, 1), (1, 0), (2, 0), (2, 1)):
            second_wait(buf, p, n, d, h)

    for p, (_, _, _, c0, cols) in enumerate(PARTS):
        put(xb[p], p, tok[:, c0 : c0 + cols])
    pl.semaphore_wait(barrier, count)
    for item in rows:
        first_start(*item)
    table, extra = route_tables(routes[...], weights[...])
    for p in range(3):
        put(qb[p], p, table)
    put(rwb, 0, extra)
    for item in tables:
        first_start(*item)
    for p, (_, _, _, c0, cols) in enumerate(PARTS):
        put(cb[p], p, cot[:, c0 : c0 + cols])
    for item in grads:
        first_start(*item)
    for load in loads:
        load.start()
    for item in rows + tables + grads:
        first_wait(*item)
        second_start(*item)
    for item in tables + rows:
        relay(*item)
    for item in tables:
        rest_wait(*item)
    for p, (_, _, slot_axis, _, _) in enumerate(PARTS):

        def build(g, _, p=p, slot_axis=slot_axis):
            st[p, g] = one_hot(qb[p][pl.ds(2 * g, 2)].reshape(256, 128), co, slot_axis)
            return 0

        lax.fori_loop(0, 4, build, 0)

    def pick(buf, out, p):
        cols = buf.shape[-1]

        def step(g, _):
            r = contract(st[p, g], buf[pl.ds(2 * g, 2)].reshape(256, cols), 0, 0)
            out[:, pl.ds(pl.multiple_of(g * 32, 32), 32), :] = r.astype(BF16).reshape(8, 32, cols)
            return 0

        lax.fori_loop(0, 4, step, 0)

    def slot_ends(p):
        axis = PARTS[p][2]
        for dc in (0, 1):
            for d in (2, 1, 3, 0):
                if dc == 0 and d == 0:
                    continue
                there, other = (co[axis] + d) % 4, (core + dc) % 2
                yield dc * 4 + d, other * 4 + there, device(moved(co, axis, there), other)

    moving = {}

    def slot_start(way, src, dst, p, n):
        me = core * 4 + co[PARTS[p][2]]
        ss, rs, loc = (s3, r3, loc3) if way == 0 else (s4, r4, loc4)
        copies = [remote(src.at[k], dst.at[me], ss.at[n, i], rs.at[n, me], to) for i, k, to in slot_ends(p)]
        for copy in copies:
            copy.start()
        local = pltpu.make_async_copy(src.at[me], dst.at[me], loc.at[n])
        local.start()
        moving[way, n] = (src, dst, p, copies, local, ss, rs)

    def slot_sent(way, n):
        for copy in moving[way, n][3]:
            copy.wait_send()
        moving[way, n][4].wait()

    def slot_got(way, n):
        src, dst, p, _, _, ss, rs = moving[way, n]
        for i, k, to in slot_ends(p):
            remote(src.at[k], dst.at[k], ss.at[n, i], rs.at[n, k], to).wait_recv()

    pick(rwb, send[6], 0)
    slot_start(0, send[6], rw, 0, 6)
    for p in range(3):
        rest_wait(*rows[p])
        pick(xb[p], send[p], p)
        landed(p)
        slot_start(0, send[p], x[p], p, p)
    for item in grads:
        relay(*item)
    for p in range(3):
        rest_wait(*grads[p])
        pick(cb[p], send[3 + p], p)
        landed(3 + p)
        slot_start(0, send[3 + p], c[p], p, 3 + p)
    for n in range(6, 10):
        landed(n)

    for n in (6, 0, 1, 2):
        slot_sent(0, n)
        slot_got(0, n)
    for load in loads:
        load.wait()

    def gather_into(acc, r, p, n0):
        for row, count, at in pieces(p):
            at = (*at, *([slice(None)] * (4 - len(at))), pl.ds(n0, 256))
            where = acc.at[at]
            piece = r[row : row + count].reshape(where.shape)
            where[...] = piece if p == 0 else where[...] + piece

    def pre(n, _):
        n0 = pl.multiple_of(n * 256, 256)
        for w, acc in ((wg, ag), (wu, au)):
            for p, (_, _, _, c0, cols) in enumerate(PARTS):
                part = x[p][...].reshape(1024, cols)
                gather_into(acc, jnp.dot(part, w[c0 : c0 + cols, pl.ds(n0, 256)], preferred_element_type=F32), p, n0)
        return 0

    lax.fori_loop(0, 3, pre, 0)

    lane = lax.broadcasted_iota(jnp.int32, (128, 128), 1)
    row = lax.broadcasted_iota(jnp.int32, (128, 128), 0)
    spread = jnp.where((row < 8) & (lane < 32) & (lane % 8 == row), 1.0, 0.0).astype(BF16)

    def weigh(k, _):
        route = jnp.dot(rw[k], spread, preferred_element_type=F32)
        taken = jnp.where((route == own) & (lane >= 8), rw[k].astype(F32), 0.0)
        wcol[k] = jnp.broadcast_to(jnp.sum(taken, axis=1, keepdims=True), (128, 128))
        return 0

    lax.fori_loop(0, 8, weigh, 0)

    def rows32(y):
        return pl.ds(pl.multiple_of(y * 32, 32), 32)

    def activate(i, _):
        k, y = i // 4, i % 4
        g, u = ag[k, y].reshape(32, 768), au[k, y].reshape(32, 768)
        w = wcol[k, rows32(y), 0:1]
        ah[k, y] = (g * jax.nn.sigmoid(g) * u * w).reshape(4, 8, 768)
        return 0

    lax.fori_loop(0, 32, activate, 0)

    def ordered(acc, out, p):
        for row, count, at in pieces(p):
            out[row : row + count, :] = acc[at].reshape(count, 768).astype(BF16)

    for p, (_, _, _, c0, cols) in enumerate(PARTS):
        ordered(ah, hw[p], p)

        def forward(n0, width, p=p, c0=c0):
            r = jnp.dot(hw[p][...], wd[:, pl.ds(c0 + n0, width)], preferred_element_type=F32)
            send[p][:, :, pl.ds(n0, width)] = r.astype(BF16).reshape(8, 128, width)

        tiles(cols, forward)
        slot_start(1, send[p], xb[p], p, p)

    for n in (3, 4, 5):
        slot_sent(0, n)
        slot_got(0, n)

    def hidden_back(n, _):
        n0 = pl.multiple_of(n * 256, 256)
        for p, (_, _, _, c0, cols) in enumerate(PARTS):
            r = contract(c[p][...].reshape(1024, cols), wd[pl.ds(n0, 256), c0 : c0 + cols], 1, 1)
            gather_into(ah, r, p, n0)
        return 0

    lax.fori_loop(0, 3, hidden_back, 0)
    lane32 = lax.broadcasted_iota(jnp.int32, (32, 128), 1)

    def derive(i, _):
        k, y = i // 4, i % 4
        g, u, h = ag[k, y].reshape(32, 768), au[k, y].reshape(32, 768), ah[k, y].reshape(32, 768)
        w = wcol[k, rows32(y), 0:1]
        s = jax.nn.sigmoid(g)
        silu = g * s
        value = jnp.sum(silu * u * h, axis=1, keepdims=True)
        high = value.astype(BF16).astype(F32)
        match = jnp.dot(rw[k, rows32(y)], spread, preferred_element_type=F32) == own
        both = jnp.where(lane32 < 8, high, jnp.where(lane32 < 16, value - high, 0.0))
        send[6][k, rows32(y)] = jnp.where(match, both, 0.0).astype(BF16)
        h = h * w
        ag[k, y] = (h * u * s * (1.0 + g * (1.0 - s))).reshape(4, 8, 768)
        au[k, y] = (h * silu).reshape(4, 8, 768)
        return 0

    lax.fori_loop(0, 32, derive, 0)
    slot_start(1, send[6], vr, 0, 6)
    for p, (_, _, _, c0, cols) in enumerate(PARTS):
        ordered(ag, gb, p)
        ordered(au, ub, p)

        def backward(n0, width, p=p, c0=c0):
            at = pl.ds(c0 + n0, width)
            r = contract(gb[...], wg[at, :], 1, 1) + contract(ub[...], wu[at, :], 1, 1)
            send[3 + p][:, :, pl.ds(n0, width)] = r.astype(BF16).reshape(8, 128, width)

        tiles(cols, backward)
        slot_start(1, send[3 + p], cb[p], p, 3 + p)

    sent = []
    back_in = [*xb, *cb, vr]

    def go(copy):
        copy.start()
        sent.append(copy)

    def ring_copy(p, n, chunk, kind):
        a2 = PARTS[p][1]
        target = device(moved(co, a2, (co[a2] + (1 if kind in (0, 2, 3) else 3)) % 4), core)
        return remote(send[n].at[chunk], ring[n].at[kind], s5.at[n, kind], r5.at[n, kind], target)

    def ring_first(p, n):
        slot_sent(1, n)
        slot_got(1, n)
        cols = send[n].shape[-1]
        me = co[PARTS[p][1]]
        for d in (2, 1, 3, 0):
            g = (me + d) % 4
            got = back_in[n][:, pl.ds(pl.multiple_of(g * 32, 32), 32), :].reshape(256, cols)
            r = jnp.dot(st[p, g], got, preferred_element_type=F32)
            send[n][pl.ds(2 * g, 2)] = r.astype(BF16).reshape(2, 128, cols)
            if d == 2:
                go(ring_copy(p, n, 2 * g, 0))
                go(ring_copy(p, n, 2 * g + 1, 1))
            if d == 1:
                go(ring_copy(p, n, 2 * g + 1, 3))
            if d == 3:
                go(ring_copy(p, n, 2 * g, 4))

    def stage(i, cols):
        return hw[0].at[128 * i : 128 * i + 128, 0:cols]

    def ring_pass(items):
        todo = []
        for i, (p, n) in enumerate(items):
            me = co[PARTS[p][1]]
            cols = send[n].shape[-1]
            for j, (chunk, out) in enumerate(((2 * ((me + 1) % 4), 2), (2 * ((me + 3) % 4) + 1, 5))):
                ring_copy(p, n, chunk, j).wait_recv()
                slot = 2 * i + j
                copy = pltpu.make_async_copy(ring[n].at[j], stage(slot, cols), ls.at[slot])
                copy.start()
                todo.append((p, n, chunk, out, copy, stage(slot, cols)))
        for p, n, chunk, out, copy, held in todo:
            copy.wait()
            send[n][chunk] = (send[n][chunk].astype(F32) + held[...].astype(F32)).astype(BF16)
            go(ring_copy(p, n, chunk, out))

    def line_first(items):
        todo = []

        def finish(p, n, copies):
            a1, a2 = PARTS[p][:2]
            for h in (0, 1):
                chunk = 2 * co[a2] + h
                total = send[n][chunk].astype(F32)
                for copy, held in copies[h]:
                    copy.wait()
                    total = total + held[...].astype(F32)
                send[n][chunk] = total.astype(BF16)
            for d in (2, 1, 3):
                i = (co[a1] + d) % 4
                chunk, at = source(p, co[a2], i)
                go(remote(
                    send[n].at[chunk, at], line[n].at[co[a1]], s6.at[n, d - 1], r6.at[n, co[a1]],
                    device(moved(co, a1, i), core),
                ))
            chunk, at = source(p, co[a2], co[a1])
            mine = pltpu.make_async_copy(send[n].at[chunk, at], line[n].at[co[a1]], s6.at[n, 3])
            mine.start()
            owns.append(mine)

        for i, (p, n) in enumerate(items):
            cols = send[n].shape[-1]
            copies = ([], [])
            for kind in (2, 3, 4, 5):
                ring_copy(p, n, 0, kind).wait_recv()
                slot = 4 * (i % 2) + kind - 2
                copy = pltpu.make_async_copy(ring[n].at[kind], stage(slot, cols), ls.at[slot])
                copy.start()
                copies[kind % 2].append((copy, stage(slot, cols)))
            todo.append((p, n, copies))
            if i:
                finish(*todo[i - 1])
        finish(*todo[-1])

    owns = []
    outs = [(p, p) for p in range(3)]
    backs = [(0, 6)] + [(p, 3 + p) for p in range(3)]
    for item in outs:
        ring_first(*item)
    for p, (_, _, _, c0, cols) in enumerate(PARTS):

        def down(n, _, p=p, c0=c0, cols=cols):
            at = pl.ds(pl.multiple_of(n * 256, 256), 256)
            wd[at, c0 : c0 + cols] = contract(hw[p][:, at], c[p][...].reshape(1024, cols), 0, 0).astype(BF16)
            return 0

        lax.fori_loop(0, 3, down, 0)
    done = [pltpu.make_async_copy(wd, dgrad, sg.at[0])]
    done[0].start()
    ring_pass(outs)
    for item in backs:
        ring_first(*item)
    line_first(outs)

    def weight_grads(p):
        c0, cols = PARTS[p][3:]

        def gate(n0, width):
            part = x[p][:, :, pl.ds(n0, width)].reshape(1024, width)
            at = pl.ds(c0 + n0, width)
            wg[at, :] = contract(part, gb[...], 0, 0).astype(BF16)
            wu[at, :] = contract(part, ub[...], 0, 0).astype(BF16)

        tiles(cols, gate)
        for i, (src, dst) in enumerate(((wg, ggrad), (wu, ugrad))):
            copy = pltpu.make_async_copy(src.at[pl.ds(c0, cols)], dst.at[pl.ds(c0, cols)], sg.at[1 + 2 * p + i])
            copy.start()
            done.append(copy)

    weight_grads(2)
    ring_pass(backs)
    ordered(ag, gb, 1)
    ordered(au, ub, 1)
    weight_grads(1)
    line_first(backs)
    ordered(ag, gb, 0)
    ordered(au, ub, 0)
    weight_grads(0)
    for p, n in outs + backs:
        a1 = PARTS[p][0]
        for d in (1, 2, 3):
            j = (co[a1] + d) % 4
            got = line[n].at[j]
            remote(got, got, s6.at[n, d - 1], r6.at[n, j], device(moved(co, a1, j), core)).wait_recv()
    for copy in sent:
        copy.wait_send()
    for copy in owns + done:
        copy.wait()


def last_kernel(*refs):
    line, grads, outs = refs[0:7], refs[7:10], refs[10:16]
    held, mixed, tgrad, vgrad = refs[16:20]
    kept, (ls, gs, hs, os) = refs[20:23], refs[23:27]
    pieces_of = []
    for i in range(3):
        part = grads[i].shape[0] // 4
        for j in range(4):
            at = pl.ds(j * part, part)
            pieces_of.append((
                pltpu.make_async_copy(grads[i].at[at], kept[i].at[at], gs.at[i, j]),
                pltpu.make_async_copy(kept[i].at[at], outs[3 + i].at[at], hs.at[i, j]),
            ))
    spans = [(c0, cols) for _, _, _, c0, cols in PARTS]
    places = [(0, *span) for span in spans] + [(1, *span) for span in spans] + [(2, 0, 128)]
    loads = [
        pltpu.make_async_copy(line[n], held.at[a, :, :, pl.ds(c0, cols)], ls.at[n])
        for n, (a, c0, cols) in enumerate(places)
    ]
    for load in loads + [first for first, _ in pieces_of]:
        load.start()
    for first, second in pieces_of:
        first.wait()
        second.start()
    for load in loads:
        load.wait()

    def total(a, at):
        return jnp.sum(held[a, :, at, :].astype(F32), axis=0)

    def step(i, _):
        at = pl.ds(pl.multiple_of(i * 16, 16), 16)
        mixed[at, :] = total(0, at).astype(BF16)
        tgrad[at, :] = total(1, at).astype(BF16)
        return 0

    lax.fori_loop(0, 4, step, 0)
    lane = lax.broadcasted_iota(jnp.int32, (8, 128), 1)
    row = lax.broadcasted_iota(jnp.int32, (8, 128), 0)
    both = jnp.where((lane < 16) & (lane % 8 == row), 1.0, 0.0).astype(BF16)
    value = jnp.sum(held[2, :, :, 0:128].astype(F32), axis=0).astype(BF16)
    vgrad[...] = contract(both, value, 1, 1)
    ends = [pltpu.make_async_copy(src, dst, os.at[i]) for i, (src, dst) in enumerate(zip((mixed, tgrad, vgrad), outs[:3], strict=True))]
    for copy in ends:
        copy.start()
    for copy in ends + [second for _, second in pieces_of]:
        copy.wait()


def per_device(tokens, routes, route_weights, cotangent, gate_weight, up_weight, down_weight):
    widths = [part[4] for part in PARTS]
    shape, dma = jax.ShapeDtypeStruct, pltpu.SemaphoreType.DMA
    any_, vmem = pl.BlockSpec(memory_space=pl.ANY), pl.BlockSpec(memory_space=pltpu.VMEM)
    items = widths * 2 + [128]
    weight_shapes = [shape((2048, 768), BF16), shape((2048, 768), BF16), shape((768, 2048), BF16)]

    def chunks(ws):
        return [pltpu.VMEM((8, 128, w), BF16) for w in ws]

    got = pl.pallas_call(
        moe_kernel,
        out_shape=weight_shapes + [shape((6, 128, w), BF16) for w in items] + [shape((4, 64, w), BF16) for w in items],
        in_specs=[vmem] * 4 + [any_] * 3,
        out_specs=[any_] * 17,
        scratch_shapes=chunks(widths * 2 + [128] * 5)
        + chunks(items)
        + chunks(items)
        + [pltpu.VMEM((3, 4, 256, 256), BF16)]
        + [pltpu.VMEM((2048, 768), BF16), pltpu.VMEM((2048, 768), BF16), pltpu.VMEM((768, 2048), BF16)]
        + [pltpu.VMEM((8, 4, 4, 8, 768), F32)] * 3
        + [pltpu.VMEM((1024, 768), BF16)] * 5
        + [pltpu.VMEM((8, 128, 128), F32)]
        + [dma((10, 3)), dma((10, 4)), dma((10, 6)), dma((10, 4, 2)), dma((7, 8)), dma((7, 8)), dma((7,)), dma((3,))]
        + [dma((7, 8)), dma((7, 8)), dma((7,)), dma((7, 6)), dma((7, 6)), dma((7, 4)), dma((7, 4)), dma((7,)), dma((8,))],
        compiler_params=pltpu.CompilerParams(collective_id=0, has_side_effects=True, vmem_limit_bytes=62 * 2**20),
    )(tokens, cotangent, routes.T, route_weights.T, gate_weight[0], up_weight[0], down_weight[0])
    mixed, token_grad, weight_grad, gate_grad, up_grad, down_grad = pl.pallas_call(
        last_kernel,
        out_shape=[shape((64, 2048), BF16), shape((64, 2048), BF16), shape((8, 64), F32)] + weight_shapes,
        in_specs=[any_] * 10,
        out_specs=[any_] * 6,
        scratch_shapes=[
            pltpu.VMEM((3, 4, 64, 2048), BF16),
            pltpu.VMEM((64, 2048), BF16),
            pltpu.VMEM((64, 2048), BF16),
            pltpu.VMEM((8, 64), F32),
            *[pltpu.VMEM(w.shape, BF16) for w in weight_shapes],
            dma((7,)),
            dma((3, 4)),
            dma((3, 4)),
            dma((3,)),
        ],
        compiler_params=pltpu.CompilerParams(vmem_limit_bytes=61 * 2**20),
    )(*got[10:17], *got[0:3])
    return (mixed, token_grad, weight_grad.T, gate_grad[None], up_grad[None], down_grad[None])


def solution(mesh):
    placed = (
        P(("node", "rail"), None),
        P(("node", "rail"), None),
        P(("node", "rail"), None),
        P(("node", "rail"), None),
        P(("node", "rail"), None, None),
        P(("node", "rail"), None, None),
        P(("node", "rail"), None, None),
    )
    return jax.shard_map(
        per_device,
        mesh=mesh,
        in_specs=placed,
        out_specs=(
            P(("node", "rail"), None),
            P(("node", "rail"), None),
            P(("node", "rail"), None),
            P(("node", "rail"), None, None),
            P(("node", "rail"), None, None),
            P(("node", "rail"), None, None),
        ),
        check_vma=False,
    )
```

```python
import jax
import jax.numpy as jnp
from jax import lax
from jax.experimental import pallas as pl
from jax.experimental.pallas import tpu as pltpu
from jax.sharding import PartitionSpec as P

MESH = pl.DeviceIdType.MESH
F32, BF16 = jnp.float32, jnp.bfloat16
PARTS = ((0, 1, 2, 0, 768), (1, 2, 0, 768, 640), (2, 0, 1, 1408, 640))


def place():
    node, rail = lax.axis_index("node"), lax.axis_index("rail")
    return (node // 2, rail % 4, rail // 4), node % 2


def moved(co, axis, value):
    return tuple(value if i == axis else v for i, v in enumerate(co))


def device(co, core):
    return (co[0] * 2 + core, co[2] * 4 + co[1])


def remote(src, dst, send, recv, target):
    return pltpu.make_async_remote_copy(
        src_ref=src, dst_ref=dst, send_sem=send, recv_sem=recv, device_id=target, device_id_type=MESH
    )


def greet(co, core):
    barrier = pltpu.get_barrier_semaphore()
    targets = [device(co, 1 - core)]
    for axis in range(3):
        for step in (1, 2, 3):
            there = moved(co, axis, (co[axis] + step) % 4)
            targets += [device(there, core), device(there, 1 - core)]
    for target in targets:
        pl.semaphore_signal(barrier, inc=1, device_id=target, device_id_type=MESH)
    return barrier, len(targets)


def one_hot(table, co, slot_axis):
    expert = lax.broadcasted_iota(jnp.int32, (128, 256), 0)
    lane = lax.broadcasted_iota(jnp.int32, (128, 256), 1)
    core, along = lane // 128, (lane // 32) % 4
    there = moved(co, slot_axis, along)
    owner = (there[0] * 2 + core) * 16 + there[2] * 4 + there[1]
    spread = jnp.dot(table, jnp.where(expert == owner, 1.0, 0.0).astype(BF16), preferred_element_type=F32)
    row = lax.broadcasted_iota(jnp.int32, (256, 256), 0)
    lane = lax.broadcasted_iota(jnp.int32, (256, 256), 1)
    wanted = jnp.where(row // 64 == (lane // 8) % 4, lane % 8 + 1, -1).astype(F32)
    return jnp.where(spread == wanted, 1.0, 0.0).astype(BF16)


def pieces(p):
    for k in range(8):
        c, d = k // 4, k % 4
        if p == 0:
            yield k * 128, 128, (k,)
        elif p == 1:
            yield k * 128, 128, (slice(4 * c, 4 * c + 4), slice(None), d)
        else:
            for x in range(4):
                yield k * 128 + x * 32, 32, (slice(4 * c, 4 * c + 4), d, x)


def tiles(cols, body):
    def step(n, _):
        body(pl.multiple_of(n * 256, 256), 256)
        return 0

    lax.fori_loop(0, cols // 256, step, 0)
    if cols % 256:
        body(cols - cols % 256, cols % 256)


def contract(a, b, da, db):
    return lax.dot_general(a, b, (((da,), (db,)), ((), ())), preferred_element_type=F32)


def route_tables(routes, weights):
    lanes = lax.broadcasted_iota(jnp.int32, (64, 128), 1).astype(F32)
    ids = routes.astype(F32).astype(BF16)
    rows8 = lax.broadcasted_iota(jnp.int32, (8, 128), 0)
    named = jnp.zeros((64, 128), F32)
    for k in range(8):
        pick = jnp.where(rows8 == k, 1.0, 0.0).astype(BF16)
        named = named + jnp.where(contract(ids, pick, 0, 0) == lanes, 1.0, 0.0)
    row = lax.broadcasted_iota(jnp.int32, (64, 64), 0)
    col = lax.broadcasted_iota(jnp.int32, (64, 64), 1)
    upto = jnp.where(col <= row, 1.0, 0.0).astype(BF16)
    counted = jnp.dot(upto, named.astype(BF16), preferred_element_type=F32)
    table = (counted * named).astype(BF16)
    high = weights.astype(BF16)
    mid = (weights - high.astype(F32)).astype(BF16)
    low = (weights - high.astype(F32) - mid.astype(F32)).astype(BF16)
    lane8 = lax.broadcasted_iota(jnp.int32, (8, 128), 1)
    extra = jnp.zeros((64, 128), F32)
    for i, part in enumerate(((routes + 1).astype(F32).astype(BF16), high, mid, low)):
        extra = extra + contract(part, jnp.where(lane8 == rows8 + 8 * i, 1.0, 0.0).astype(BF16), 0, 0)
    return table, extra.astype(BF16)


def moe_kernel(tok, cot, routes, weights, wgi, wui, wdi, *refs):
    wg, wu, wd = refs[0:3]
    ring, line = refs[3:10], refs[10:17]
    refs = refs[17:]
    xb, cb, vr, qb, rwb = refs[0:3], refs[3:6], refs[6], refs[7:10], refs[10]
    send = refs[11:18]
    x, c, rw, st = refs[18:21], refs[21:24], refs[24], refs[25]
    ag, au, ah = refs[26:29]
    hw, gb, ub, wcol, rep = refs[29:32], refs[32], refs[33], refs[34], refs[35]
    s1, r1, s2, r2, s3, r3, loc3, ld, s4, r4, loc4, s5, r5, s6, r6, ls = refs[36:52]
    co, core = place()
    own = ((co[0] * 2 + core) * 16 + co[2] * 4 + co[1] + 1).astype(F32)
    barrier, count = greet(co, core)
    loads = [pltpu.make_async_copy(src, dst, ld.at[i]) for i, (src, dst) in enumerate(((wgi, wg), (wui, wu), (wdi, wd)))]

    def half_rows(i):
        return pl.ds(pl.multiple_of((i % 2) * 64, 64), 64)

    def source(p, i2, i1):
        return 2 * i2 + i1 // 2, half_rows(i1)

    rows = [(xb[p], p, p) for p in range(3)]
    grads = [(cb[p], p, 3 + p) for p in range(3)]
    tables = [(qb[p], p, 6 + p) for p in range(3)] + [(rwb, 1, 9)]

    def put(buf, p, value):
        a1, a2 = PARTS[p][:2]
        chunk, at = source(p, co[a2], co[a1])
        buf[chunk, at] = value

    flying = {}

    def launch(n, copies):
        for copy in copies:
            copy.start()
        flying.setdefault(n, []).extend(copies)

    def landed(n):
        for copy in flying.pop(n):
            copy.wait_send()

    def first_start(buf, p, n):
        a1, a2 = PARTS[p][:2]
        chunk, at = source(p, co[a2], co[a1])
        mine = buf.at[chunk, at]
        launch(n, [
            remote(mine, mine, s1.at[n, d - 1], r1.at[n, co[a1]], device(moved(co, a1, (co[a1] + d) % 4), core))
            for d in (2, 1, 3)
        ])

    def first_wait(buf, p, n):
        a1, a2 = PARTS[p][:2]
        for d in (1, 2, 3):
            i = (co[a1] + d) % 4
            chunk, at = source(p, co[a2], i)
            got = buf.at[chunk, at]
            remote(got, got, s1.at[n, d - 1], r1.at[n, i], device(moved(co, a1, i), core)).wait_recv()

    def second_copy(buf, p, n, block, h, right, number):
        a2 = PARTS[p][1]
        part = buf.at[2 * block + h]
        target = device(moved(co, a2, (co[a2] + (1 if right else 3)) % 4), core)
        return remote(part, part, s2.at[n, number], r2.at[n, block, h], target)

    def second_start(buf, p, n):
        me = co[PARTS[p][1]]
        launch(n, [
            second_copy(buf, p, n, me, 0, True, 0),
            second_copy(buf, p, n, me, 1, False, 1),
            second_copy(buf, p, n, me, 1, True, 2),
            second_copy(buf, p, n, me, 0, False, 3),
        ])

    def second_wait(buf, p, n, d, h):
        second_copy(buf, p, n, (co[PARTS[p][1]] + d) % 4, h, True, 0).wait_recv()

    def relay(buf, p, n):
        me = co[PARTS[p][1]]
        second_wait(buf, p, n, 3, 0)
        launch(n, [second_copy(buf, p, n, (me + 3) % 4, 0, True, 4)])
        second_wait(buf, p, n, 1, 1)
        launch(n, [second_copy(buf, p, n, (me + 1) % 4, 1, False, 5)])

    def rest_wait(buf, p, n):
        for d, h in ((3, 1), (1, 0), (2, 0), (2, 1)):
            second_wait(buf, p, n, d, h)

    for p, (_, _, _, c0, cols) in enumerate(PARTS):
        put(xb[p], p, tok[:, c0 : c0 + cols])
    pl.semaphore_wait(barrier, count)
    for item in rows:
        first_start(*item)
    table, extra = route_tables(routes[...], weights[...])
    for p in range(3):
        put(qb[p], p, table)
    put(rwb, 1, extra)
    for item in tables:
        first_start(*item)
    for p, (_, _, _, c0, cols) in enumerate(PARTS):
        put(cb[p], p, cot[:, c0 : c0 + cols])
    for item in grads:
        first_start(*item)
    for load in loads:
        load.start()
    for item in rows + tables + grads:
        first_wait(*item)
        second_start(*item)
    for item in rows + tables + grads:
        relay(*item)
    for item in tables:
        rest_wait(*item)
    for p, (_, _, slot_axis, _, _) in enumerate(PARTS):

        def build(g, _, p=p, slot_axis=slot_axis):
            st[p, g] = one_hot(qb[p][pl.ds(2 * g, 2)].reshape(256, 128), co, slot_axis)
            return 0

        lax.fori_loop(0, 4, build, 0)

    def pick(buf, out, p):
        cols = buf.shape[-1]

        def step(g, _):
            r = contract(st[p, g], buf[pl.ds(2 * g, 2)].reshape(256, cols), 0, 0)
            out[:, pl.ds(pl.multiple_of(g * 32, 32), 32), :] = r.astype(BF16).reshape(8, 32, cols)
            return 0

        lax.fori_loop(0, 4, step, 0)

    def slot_ends(p):
        axis = PARTS[p][2]
        for dc in (0, 1):
            for d in (2, 1, 3, 0):
                if dc == 0 and d == 0:
                    continue
                there, other = (co[axis] + d) % 4, (core + dc) % 2
                yield dc * 4 + d, other * 4 + there, device(moved(co, axis, there), other)

    moving = {}

    def slot_start(way, src, dst, p, n):
        me = core * 4 + co[PARTS[p][2]]
        ss, rs, loc = (s3, r3, loc3) if way == 0 else (s4, r4, loc4)
        copies = [remote(src.at[k], dst.at[me], ss.at[n, i], rs.at[n, me], to) for i, k, to in slot_ends(p)]
        for copy in copies:
            copy.start()
        local = pltpu.make_async_copy(src.at[me], dst.at[me], loc.at[n])
        local.start()
        moving[way, n] = (src, dst, p, copies, local, ss, rs)

    def slot_sent(way, n):
        for copy in moving[way, n][3]:
            copy.wait_send()
        moving[way, n][4].wait()

    def slot_got(way, n):
        src, dst, p, _, _, ss, rs = moving[way, n]
        for i, k, to in slot_ends(p):
            remote(src.at[k], dst.at[k], ss.at[n, i], rs.at[n, k], to).wait_recv()

    pick(rwb, send[6], 1)
    slot_start(0, send[6], rw, 1, 6)
    for p in range(3):
        rest_wait(*rows[p])
        pick(xb[p], send[p], p)
        landed(p)
        slot_start(0, send[p], x[p], p, p)
    for p in range(3):
        rest_wait(*grads[p])
        pick(cb[p], send[3 + p], p)
        landed(3 + p)
        slot_start(0, send[3 + p], c[p], p, 3 + p)
    for n in range(6, 10):
        landed(n)

    for n in (6, 0, 1, 2):
        slot_sent(0, n)
        slot_got(0, n)
    for load in loads:
        load.wait()

    def gather_into(acc, r, p, n0):
        for row, count, at in pieces(p):
            at = (*at, *([slice(None)] * (4 - len(at))), pl.ds(n0, 256))
            where = acc.at[at]
            piece = r[row : row + count].reshape(where.shape)
            where[...] = piece if p == 0 else where[...] + piece

    def pre(n, _):
        n0 = pl.multiple_of(n * 256, 256)
        for w, acc in ((wg, ag), (wu, au)):
            for p, (_, _, _, c0, cols) in enumerate(PARTS):
                part = x[p][...].reshape(1024, cols)
                gather_into(acc, jnp.dot(part, w[c0 : c0 + cols, pl.ds(n0, 256)], preferred_element_type=F32), p, n0)
        return 0

    lax.fori_loop(0, 3, pre, 0)

    lane = lax.broadcasted_iota(jnp.int32, (128, 128), 1)
    row = lax.broadcasted_iota(jnp.int32, (128, 128), 0)
    spread = jnp.where((row < 8) & (lane < 32) & (lane % 8 == row), 1.0, 0.0).astype(BF16)

    for start, count, at in pieces(1):
        extra = rw[start // 128]
        route = jnp.dot(extra, spread, preferred_element_type=F32)
        taken = jnp.where((route == own) & (lane >= 8), extra.astype(F32), 0.0)
        wcol[at] = jnp.broadcast_to(jnp.sum(taken, axis=1, keepdims=True), (128, 128)).reshape(4, 4, 8, 128)
        rep[at] = route.reshape(4, 4, 8, 128)

    def activate(i, _):
        k, y = i // 4, i % 4
        g, u = ag[k, y].reshape(32, 768), au[k, y].reshape(32, 768)
        w = wcol[k, y].reshape(32, 128)[:, 0:1]
        s = jax.nn.sigmoid(g)
        silu = g * s * w
        hidden = silu * u
        ah[k, y] = hidden.reshape(4, 8, 768)
        hw[0][pl.ds(pl.multiple_of(i * 32, 32), 32), :] = hidden.astype(BF16)
        ag[k, y] = (u * s * w * (1.0 + g * (1.0 - s))).reshape(4, 8, 768)
        au[k, y] = silu.reshape(4, 8, 768)
        return 0

    lax.fori_loop(0, 32, activate, 0)

    def ordered(acc, out, p):
        for row, count, at in pieces(p):
            out[row : row + count, :] = acc[at].reshape(count, 768).astype(BF16)

    for p, (_, _, _, c0, cols) in enumerate(PARTS):
        if p:
            ordered(ah, hw[p], p)

        def forward(n0, width, p=p, c0=c0):
            r = jnp.dot(hw[p][...], wd[:, pl.ds(c0 + n0, width)], preferred_element_type=F32)
            send[p][:, :, pl.ds(n0, width)] = r.astype(BF16).reshape(8, 128, width)

        tiles(cols, forward)
        slot_start(1, send[p], xb[p], p, p)

    for n in (3, 4, 5):
        slot_sent(0, n)
        slot_got(0, n)

    def hidden_back(n, _):
        n0 = pl.multiple_of(n * 256, 256)
        for p, (_, _, _, c0, cols) in enumerate(PARTS):
            r = contract(c[p][...].reshape(1024, cols), wd[pl.ds(n0, 256), c0 : c0 + cols], 1, 1)
            gather_into(ah, r, p, n0)
        return 0

    lax.fori_loop(0, 3, hidden_back, 0)
    lane32 = lax.broadcasted_iota(jnp.int32, (32, 128), 1)

    def derive(i, _):
        k, y = i // 4, i % 4
        at = pl.ds(pl.multiple_of(i * 32, 32), 32)
        h = ah[k, y].reshape(32, 768)
        gate, up = h * ag[k, y].reshape(32, 768), h * au[k, y].reshape(32, 768)
        ag[k, y], au[k, y] = gate.reshape(4, 8, 768), up.reshape(4, 8, 768)
        gb[at, :], ub[at, :] = gate.astype(BF16), up.astype(BF16)
        w = wcol[k, y].reshape(32, 128)
        value = jnp.sum(hw[0][at, :].astype(F32) * h, axis=1, keepdims=True) / w
        high = value.astype(BF16).astype(F32)
        both = jnp.where(lane32 < 8, high, jnp.where(lane32 < 16, value - high, 0.0))
        rep[k, y] = jnp.where(rep[k, y].reshape(32, 128) == own, both, 0.0).reshape(4, 8, 128)
        return 0

    lax.fori_loop(0, 32, derive, 0)
    for start, count, at in pieces(1):
        send[6][start // 128] = rep[at].reshape(128, 128).astype(BF16)
    slot_start(1, send[6], vr, 1, 6)
    for p, (_, _, _, c0, cols) in enumerate(PARTS):
        if p:
            ordered(ag, gb, p)
            ordered(au, ub, p)

        def backward(n0, width, p=p, c0=c0):
            at = pl.ds(c0 + n0, width)
            r = contract(gb[...], wg[at, :], 1, 1) + contract(ub[...], wu[at, :], 1, 1)
            send[3 + p][:, :, pl.ds(n0, width)] = r.astype(BF16).reshape(8, 128, width)

        tiles(cols, backward)
        slot_start(1, send[3 + p], cb[p], p, 3 + p)

    sent = []
    back_in = [*xb, *cb, vr]

    def go(copy):
        copy.start()
        sent.append(copy)

    def ring_copy(p, n, chunk, kind):
        a2 = PARTS[p][1]
        target = device(moved(co, a2, (co[a2] + (1 if kind in (0, 2, 3) else 3)) % 4), core)
        return remote(send[n].at[chunk], ring[n].at[kind], s5.at[n, kind], r5.at[n, kind], target)

    def ring_first(p, n):
        slot_sent(1, n)
        slot_got(1, n)
        cols = send[n].shape[-1]
        me = co[PARTS[p][1]]
        for d in (2, 1, 3, 0):
            g = (me + d) % 4
            got = back_in[n][:, pl.ds(pl.multiple_of(g * 32, 32), 32), :].reshape(256, cols)
            r = jnp.dot(st[p, g], got, preferred_element_type=F32)
            send[n][pl.ds(2 * g, 2)] = r.astype(BF16).reshape(2, 128, cols)
            if d == 2:
                go(ring_copy(p, n, 2 * g, 0))
                go(ring_copy(p, n, 2 * g + 1, 1))
            if d == 1:
                go(ring_copy(p, n, 2 * g + 1, 3))
            if d == 3:
                go(ring_copy(p, n, 2 * g, 4))

    def stage(i, cols):
        return hw[0].at[128 * i : 128 * i + 128, 0:cols]

    def ring_pass(items):
        todo = []
        for i, (p, n) in enumerate(items):
            me = co[PARTS[p][1]]
            cols = send[n].shape[-1]
            for j, (chunk, out) in enumerate(((2 * ((me + 1) % 4), 2), (2 * ((me + 3) % 4) + 1, 5))):
                ring_copy(p, n, chunk, j).wait_recv()
                slot = 2 * i + j
                copy = pltpu.make_async_copy(ring[n].at[j], stage(slot, cols), ls.at[slot])
                copy.start()
                todo.append((p, n, chunk, out, copy, stage(slot, cols)))
        for p, n, chunk, out, copy, held in todo:
            copy.wait()
            send[n][chunk] = (send[n][chunk].astype(F32) + held[...].astype(F32)).astype(BF16)
            go(ring_copy(p, n, chunk, out))

    def line_first(items):
        todo = []

        def finish(p, n, copies):
            a1, a2 = PARTS[p][:2]
            for h in (0, 1):
                chunk = 2 * co[a2] + h
                total = send[n][chunk].astype(F32)
                for copy, held in copies[h]:
                    copy.wait()
                    total = total + held[...].astype(F32)
                send[n][chunk] = total.astype(BF16)
            for d in (2, 1, 3):
                i = (co[a1] + d) % 4
                chunk, at = source(p, co[a2], i)
                go(remote(
                    send[n].at[chunk, at], line[n].at[co[a1]], s6.at[n, d - 1], r6.at[n, co[a1]],
                    device(moved(co, a1, i), core),
                ))
            chunk, at = source(p, co[a2], co[a1])
            mine = pltpu.make_async_copy(send[n].at[chunk, at], line[n].at[co[a1]], s6.at[n, 3])
            mine.start()
            owns.append(mine)

        for i, (p, n) in enumerate(items):
            cols = send[n].shape[-1]
            copies = ([], [])
            for kind in (2, 3, 4, 5):
                ring_copy(p, n, 0, kind).wait_recv()
                slot = 4 * (i % 2) + kind - 2
                copy = pltpu.make_async_copy(ring[n].at[kind], stage(slot, cols), ls.at[slot])
                copy.start()
                copies[kind % 2].append((copy, stage(slot, cols)))
            todo.append((p, n, copies))
            if i:
                finish(*todo[i - 1])
        finish(*todo[-1])

    owns = []
    outs = [(p, p) for p in range(3)]
    backs = [(1, 6)] + [(p, 3 + p) for p in range(3)]
    for item in outs:
        ring_first(*item)
    for p, (_, _, _, c0, cols) in enumerate(PARTS):

        def down(n, _, p=p, c0=c0, cols=cols):
            at = pl.ds(pl.multiple_of(n * 256, 256), 256)
            wd[at, c0 : c0 + cols] = contract(hw[p][:, at], c[p][...].reshape(1024, cols), 0, 0).astype(BF16)
            return 0

        lax.fori_loop(0, 3, down, 0)

    def weight_grads(p):
        c0, cols = PARTS[p][3:]

        def gate(n0, width):
            part = x[p][:, :, pl.ds(n0, width)].reshape(1024, width)
            at = pl.ds(c0 + n0, width)
            wg[at, :] = contract(part, gb[...], 0, 0).astype(BF16)
            wu[at, :] = contract(part, ub[...], 0, 0).astype(BF16)

        tiles(cols, gate)

    weight_grads(2)
    for item in backs:
        ring_first(*item)
    ordered(ag, gb, 1)
    ordered(au, ub, 1)
    weight_grads(1)
    ring_pass(outs)
    ordered(ag, gb, 0)
    ordered(au, ub, 0)
    weight_grads(0)
    ring_pass(backs)
    line_first(outs)
    line_first(backs)
    for p, n in outs + backs:
        a1 = PARTS[p][0]
        for d in (1, 2, 3):
            j = (co[a1] + d) % 4
            got = line[n].at[j]
            remote(got, got, s6.at[n, d - 1], r6.at[n, j], device(moved(co, a1, j), core)).wait_recv()
    for copy in sent:
        copy.wait_send()
    for copy in owns:
        copy.wait()


def last_kernel(*refs):
    line, grads, outs = refs[0:7], refs[7:10], refs[10:16]
    held, mixed, tgrad, vgrad = refs[16:20]
    ls, hs, os = refs[20:23]
    copies = []
    for i in range(3):
        part = grads[i].shape[0] // 4
        for j in range(4):
            at = pl.ds(j * part, part)
            copies.append(pltpu.make_async_copy(grads[i].at[at], outs[3 + i].at[at], hs.at[i, j]))
    spans = [(c0, cols) for _, _, _, c0, cols in PARTS]
    places = [(0, *span) for span in spans] + [(1, *span) for span in spans] + [(2, 0, 128)]
    loads = [
        pltpu.make_async_copy(line[n], held.at[a, :, :, pl.ds(c0, cols)], ls.at[n])
        for n, (a, c0, cols) in enumerate(places)
    ]
    for load in loads + copies:
        load.start()
    for load in loads:
        load.wait()

    def total(a, at):
        return jnp.sum(held[a, :, at, :].astype(F32), axis=0)

    def step(i, _):
        at = pl.ds(pl.multiple_of(i * 16, 16), 16)
        mixed[at, :] = total(0, at).astype(BF16)
        tgrad[at, :] = total(1, at).astype(BF16)
        return 0

    lax.fori_loop(0, 4, step, 0)
    lane = lax.broadcasted_iota(jnp.int32, (8, 128), 1)
    row = lax.broadcasted_iota(jnp.int32, (8, 128), 0)
    both = jnp.where((lane < 16) & (lane % 8 == row), 1.0, 0.0).astype(BF16)
    value = jnp.sum(held[2, :, :, 0:128].astype(F32), axis=0).astype(BF16)
    vgrad[...] = contract(both, value, 1, 1)
    ends = [pltpu.make_async_copy(src, dst, os.at[i]) for i, (src, dst) in enumerate(zip((mixed, tgrad, vgrad), outs[:3], strict=True))]
    for copy in ends:
        copy.start()
    for copy in ends + copies:
        copy.wait()


def per_device(tokens, routes, route_weights, cotangent, gate_weight, up_weight, down_weight):
    widths = [part[4] for part in PARTS]
    shape, dma = jax.ShapeDtypeStruct, pltpu.SemaphoreType.DMA
    any_, vmem = pl.BlockSpec(memory_space=pl.ANY), pl.BlockSpec(memory_space=pltpu.VMEM)
    items = widths * 2 + [128]
    weight_shapes = [shape((2048, 768), BF16), shape((2048, 768), BF16), shape((768, 2048), BF16)]

    def chunks(ws):
        return [pltpu.VMEM((8, 128, w), BF16) for w in ws]

    got = pl.pallas_call(
        moe_kernel,
        out_shape=[pltpu.VMEM(w.shape, BF16) for w in weight_shapes] + [shape((6, 128, w), BF16) for w in items] + [shape((4, 64, w), BF16) for w in items],
        in_specs=[vmem] * 4 + [any_] * 3,
        out_specs=[vmem] * 3 + [any_] * 14,
        scratch_shapes=chunks(widths * 2 + [128] * 5)
        + chunks(items)
        + chunks(items)
        + [pltpu.VMEM((3, 4, 256, 256), BF16)]
        + [pltpu.VMEM((8, 4, 4, 8, 768), F32)] * 3
        + [pltpu.VMEM((1024, 768), BF16)] * 5
        + [pltpu.VMEM((8, 4, 4, 8, 128), F32)] * 2
        + [dma((10, 3)), dma((10, 4)), dma((10, 6)), dma((10, 4, 2)), dma((7, 8)), dma((7, 8)), dma((7,)), dma((3,))]
        + [dma((7, 8)), dma((7, 8)), dma((7,)), dma((7, 6)), dma((7, 6)), dma((7, 4)), dma((7, 4)), dma((8,))],
        compiler_params=pltpu.CompilerParams(collective_id=0, has_side_effects=True, vmem_limit_bytes=53 * 2**20),
    )(tokens, cotangent, routes.T, route_weights.T, gate_weight[0], up_weight[0], down_weight[0])
    mixed, token_grad, weight_grad, gate_grad, up_grad, down_grad = pl.pallas_call(
        last_kernel,
        out_shape=[shape((64, 2048), BF16), shape((64, 2048), BF16), shape((8, 64), F32)] + weight_shapes,
        in_specs=[any_] * 10,
        out_specs=[any_] * 6,
        scratch_shapes=[
            pltpu.VMEM((3, 4, 64, 2048), BF16),
            pltpu.VMEM((64, 2048), BF16),
            pltpu.VMEM((64, 2048), BF16),
            pltpu.VMEM((8, 64), F32),
            dma((7,)),
            dma((3, 4)),
            dma((3,)),
        ],
        compiler_params=pltpu.CompilerParams(vmem_limit_bytes=16 * 2**20),
    )(*[pltpu.with_memory_space_constraint(g, pltpu.HBM) for g in got[10:17]], *[pltpu.with_memory_space_constraint(g, pltpu.VMEM) for g in got[0:3]])
    return (mixed, token_grad, weight_grad.T, gate_grad[None], up_grad[None], down_grad[None])


def solution(mesh):
    placed = (
        P(("node", "rail"), None),
        P(("node", "rail"), None),
        P(("node", "rail"), None),
        P(("node", "rail"), None),
        P(("node", "rail"), None, None),
        P(("node", "rail"), None, None),
        P(("node", "rail"), None, None),
    )
    return jax.shard_map(
        per_device,
        mesh=mesh,
        in_specs=placed,
        out_specs=(
            P(("node", "rail"), None),
            P(("node", "rail"), None),
            P(("node", "rail"), None),
            P(("node", "rail"), None, None),
            P(("node", "rail"), None, None),
            P(("node", "rail"), None, None),
        ),
        check_vma=False,
    )
```

```python
import jax
import jax.numpy as jnp
from jax import lax
from jax.experimental import pallas as pl
from jax.experimental.pallas import tpu as pltpu
from jax.sharding import PartitionSpec as P

MESH = pl.DeviceIdType.MESH
F32, BF16 = jnp.float32, jnp.bfloat16
PARTS = ((0, 1, 2, 0, 768), (1, 2, 0, 768, 640), (2, 0, 1, 1408, 640))


def place():
    node, rail = lax.axis_index("node"), lax.axis_index("rail")
    return (node // 2, rail % 4, rail // 4), node % 2


def moved(co, axis, value):
    return tuple(value if i == axis else v for i, v in enumerate(co))


def device(co, core):
    return (co[0] * 2 + core, co[2] * 4 + co[1])


def remote(src, dst, send, recv, target):
    return pltpu.make_async_remote_copy(
        src_ref=src, dst_ref=dst, send_sem=send, recv_sem=recv, device_id=target, device_id_type=MESH
    )


def greet(co, core):
    barrier = pltpu.get_barrier_semaphore()
    targets = [device(co, 1 - core)]
    for axis in range(3):
        for step in (1, 2, 3):
            there = moved(co, axis, (co[axis] + step) % 4)
            targets += [device(there, core), device(there, 1 - core)]
    for target in targets:
        pl.semaphore_signal(barrier, inc=1, device_id=target, device_id_type=MESH)
    return barrier, len(targets)


def one_hot(table, co, slot_axis):
    expert = lax.broadcasted_iota(jnp.int32, (128, 256), 0)
    lane = lax.broadcasted_iota(jnp.int32, (128, 256), 1)
    core, along = lane // 128, (lane // 32) % 4
    there = moved(co, slot_axis, along)
    owner = (there[0] * 2 + core) * 16 + there[2] * 4 + there[1]
    spread = jnp.dot(table, jnp.where(expert == owner, 1.0, 0.0).astype(BF16), preferred_element_type=F32)
    row = lax.broadcasted_iota(jnp.int32, (256, 256), 0)
    lane = lax.broadcasted_iota(jnp.int32, (256, 256), 1)
    wanted = jnp.where(row // 64 == (lane // 8) % 4, lane % 8 + 1, -1).astype(F32)
    return jnp.where(spread == wanted, 1.0, 0.0).astype(BF16)


def pieces(p):
    for k in range(8):
        c, d = k // 4, k % 4
        if p == 0:
            yield k * 128, 128, (k,)
        elif p == 1:
            yield k * 128, 128, (slice(4 * c, 4 * c + 4), slice(None), d)
        else:
            for x in range(4):
                yield k * 128 + x * 32, 32, (slice(4 * c, 4 * c + 4), d, x)


def tiles(cols, body):
    def step(n, _):
        body(pl.multiple_of(n * 256, 256), 256)
        return 0

    lax.fori_loop(0, cols // 256, step, 0)
    if cols % 256:
        body(cols - cols % 256, cols % 256)


def contract(a, b, da, db):
    return lax.dot_general(a, b, (((da,), (db,)), ((), ())), preferred_element_type=F32)


def route_tables(routes, weights):
    lanes = lax.broadcasted_iota(jnp.int32, (64, 128), 1).astype(F32)
    ids = routes.astype(F32).astype(BF16)
    rows8 = lax.broadcasted_iota(jnp.int32, (8, 128), 0)
    named = jnp.zeros((64, 128), F32)
    for k in range(8):
        pick = jnp.where(rows8 == k, 1.0, 0.0).astype(BF16)
        named = named + jnp.where(contract(ids, pick, 0, 0) == lanes, 1.0, 0.0)
    row = lax.broadcasted_iota(jnp.int32, (64, 64), 0)
    col = lax.broadcasted_iota(jnp.int32, (64, 64), 1)
    upto = jnp.where(col <= row, 1.0, 0.0).astype(BF16)
    counted = jnp.dot(upto, named.astype(BF16), preferred_element_type=F32)
    table = (counted * named).astype(BF16)
    high = weights.astype(BF16)
    mid = (weights - high.astype(F32)).astype(BF16)
    low = (weights - high.astype(F32) - mid.astype(F32)).astype(BF16)
    lane8 = lax.broadcasted_iota(jnp.int32, (8, 128), 1)
    extra = jnp.zeros((64, 128), F32)
    for i, part in enumerate(((routes + 1).astype(F32).astype(BF16), high, mid, low)):
        extra = extra + contract(part, jnp.where(lane8 == rows8 + 8 * i, 1.0, 0.0).astype(BF16), 0, 0)
    return table, extra.astype(BF16)


def moe_kernel(tok, cot, routes, weights, wgi, wui, wdi, *refs):
    wg, wu, wd = refs[0:3]
    ring, line = refs[3:10], refs[10:17]
    refs = refs[17:]
    xb, cb, vr, qb, rwb = refs[0:3], refs[3:6], refs[6], refs[7:10], refs[10]
    send = refs[11:18]
    x, c, rw, st = refs[18:21], refs[21:24], refs[24], refs[25]
    ag, au, ah = refs[26:29]
    hw, gb, ub, wcol, rep = refs[29:32], refs[32], refs[33], refs[34], refs[35]
    s1, r1, s2, r2, s3, r3, loc3, ld, s4, r4, loc4, s5, r5, s6, r6, ls = refs[36:52]
    co, core = place()
    own = ((co[0] * 2 + core) * 16 + co[2] * 4 + co[1] + 1).astype(F32)
    barrier, count = greet(co, core)
    loads = [pltpu.make_async_copy(src, dst, ld.at[i]) for i, (src, dst) in enumerate(((wgi, wg), (wui, wu), (wdi, wd)))]

    def half_rows(i):
        return pl.ds(pl.multiple_of((i % 2) * 64, 64), 64)

    def source(p, i2, i1):
        return 2 * i2 + i1 // 2, half_rows(i1)

    rows = [(xb[p], p, p) for p in range(3)]
    grads = [(cb[p], p, 3 + p) for p in range(3)]
    tables = [(qb[p], p, 6 + p) for p in range(3)] + [(rwb, 1, 9)]

    def put(buf, p, value):
        a1, a2 = PARTS[p][:2]
        chunk, at = source(p, co[a2], co[a1])
        buf[chunk, at] = value

    flying = {}

    def launch(n, copies):
        for copy in copies:
            copy.start()
        flying.setdefault(n, []).extend(copies)

    def landed(n):
        for copy in flying.pop(n):
            copy.wait_send()

    def first_start(buf, p, n):
        a1, a2 = PARTS[p][:2]
        chunk, at = source(p, co[a2], co[a1])
        mine = buf.at[chunk, at]
        launch(n, [
            remote(mine, mine, s1.at[n, d - 1], r1.at[n, co[a1]], device(moved(co, a1, (co[a1] + d) % 4), core))
            for d in (2, 1, 3)
        ])

    def first_wait(buf, p, n):
        a1, a2 = PARTS[p][:2]
        for d in (1, 2, 3):
            i = (co[a1] + d) % 4
            chunk, at = source(p, co[a2], i)
            got = buf.at[chunk, at]
            remote(got, got, s1.at[n, d - 1], r1.at[n, i], device(moved(co, a1, i), core)).wait_recv()

    def second_copy(buf, p, n, block, h, right, number):
        a2 = PARTS[p][1]
        part = buf.at[2 * block + h]
        target = device(moved(co, a2, (co[a2] + (1 if right else 3)) % 4), core)
        return remote(part, part, s2.at[n, number], r2.at[n, block, h], target)

    def second_start(buf, p, n):
        me = co[PARTS[p][1]]
        launch(n, [
            second_copy(buf, p, n, me, 0, True, 0),
            second_copy(buf, p, n, me, 1, False, 1),
            second_copy(buf, p, n, me, 1, True, 2),
            second_copy(buf, p, n, me, 0, False, 3),
        ])

    def second_wait(buf, p, n, d, h):
        second_copy(buf, p, n, (co[PARTS[p][1]] + d) % 4, h, True, 0).wait_recv()

    def relay(buf, p, n):
        me = co[PARTS[p][1]]
        second_wait(buf, p, n, 3, 0)
        launch(n, [second_copy(buf, p, n, (me + 3) % 4, 0, True, 4)])
        second_wait(buf, p, n, 1, 1)
        launch(n, [second_copy(buf, p, n, (me + 1) % 4, 1, False, 5)])

    def near_wait(buf, p, n):
        second_wait(buf, p, n, 3, 1)
        second_wait(buf, p, n, 1, 0)

    def far_wait(buf, p, n):
        second_wait(buf, p, n, 2, 0)
        second_wait(buf, p, n, 2, 1)

    def build(p, d):
        g = (co[PARTS[p][1]] + d) % 4
        st[p, g] = one_hot(qb[p][pl.ds(2 * g, 2)].reshape(256, 128), co, PARTS[p][2])

    def pick(buf, out, p, d):
        cols = buf.shape[-1]
        g = (co[PARTS[p][1]] + d) % 4
        r = contract(st[p, g], buf[pl.ds(2 * g, 2)].reshape(256, cols), 0, 0)
        out[:, pl.ds(pl.multiple_of(g * 32, 32), 32), :] = r.astype(BF16).reshape(8, 32, cols)

    for p, (_, _, _, c0, cols) in enumerate(PARTS):
        put(xb[p], p, tok[:, c0 : c0 + cols])
    pl.semaphore_wait(barrier, count)
    for item in rows:
        first_start(*item)
    table, extra = route_tables(routes[...], weights[...])
    for p in range(3):
        put(qb[p], p, table)
    put(rwb, 1, extra)
    for item in tables:
        first_start(*item)
    for p, (_, _, _, c0, cols) in enumerate(PARTS):
        put(cb[p], p, cot[:, c0 : c0 + cols])
    for item in grads:
        first_start(*item)
    for load in loads:
        load.start()
    for item in rows + tables + grads:
        first_wait(*item)
        second_start(*item)
    def slot_ends(p):
        axis = PARTS[p][2]
        for dc in (0, 1):
            for d in (2, 1, 3, 0):
                if dc == 0 and d == 0:
                    continue
                there, other = (co[axis] + d) % 4, (core + dc) % 2
                yield dc * 4 + d, other * 4 + there, device(moved(co, axis, there), other)

    moving = {}

    def slot_start(way, src, dst, p, n):
        me = core * 4 + co[PARTS[p][2]]
        ss, rs, loc = (s3, r3, loc3) if way == 0 else (s4, r4, loc4)
        copies = [remote(src.at[k], dst.at[me], ss.at[n, i], rs.at[n, me], to) for i, k, to in slot_ends(p)]
        for copy in copies:
            copy.start()
        local = pltpu.make_async_copy(src.at[me], dst.at[me], loc.at[n])
        local.start()
        moving[way, n] = (src, dst, p, copies, local, ss, rs)

    def slot_sent(way, n):
        for copy in moving[way, n][3]:
            copy.wait_send()
        moving[way, n][4].wait()

    def slot_got(way, n):
        src, dst, p, _, _, ss, rs = moving[way, n]
        for i, k, to in slot_ends(p):
            remote(src.at[k], dst.at[k], ss.at[n, i], rs.at[n, k], to).wait_recv()

    for p in range(3):
        build(p, 0)
    pick(rwb, send[6], 1, 0)
    for p in range(3):
        pick(xb[p], send[p], p, 0)
    for item in rows + tables + grads:
        relay(*item)
    for item in tables:
        near_wait(*item)
    for p in range(3):
        build(p, 1)
        build(p, 3)
    for p in range(3):
        near_wait(*rows[p])
        pick(xb[p], send[p], p, 1)
        pick(xb[p], send[p], p, 3)
    pick(rwb, send[6], 1, 1)
    pick(rwb, send[6], 1, 3)
    for item in tables:
        far_wait(*item)
    for p in range(3):
        build(p, 2)
    for p in range(3):
        far_wait(*rows[p])
        pick(xb[p], send[p], p, 2)
        landed(p)
        slot_start(0, send[p], x[p], p, p)
    pick(rwb, send[6], 1, 2)
    slot_start(0, send[6], rw, 1, 6)
    for p in range(3):
        near_wait(*grads[p])
        for d in (0, 1, 3):
            pick(cb[p], send[3 + p], p, d)
    for p in range(3):
        far_wait(*grads[p])
        pick(cb[p], send[3 + p], p, 2)
        landed(3 + p)
        slot_start(0, send[3 + p], c[p], p, 3 + p)
    for n in range(6, 10):
        landed(n)

    for load in loads:
        load.wait()

    def gather_into(acc, r, p, n0):
        for row, count, at in pieces(p):
            at = (*at, *([slice(None)] * (4 - len(at))), pl.ds(n0, 256))
            where = acc.at[at]
            piece = r[row : row + count].reshape(where.shape)
            where[...] = piece if p == 2 else where[...] + piece

    for p in (2, 1, 0):
        c0, cols = PARTS[p][3:]
        slot_sent(0, p)
        slot_got(0, p)

        def pre(n, _, p=p, c0=c0, cols=cols):
            n0 = pl.multiple_of(n * 256, 256)
            for w, acc in ((wg, ag), (wu, au)):
                part = x[p][...].reshape(1024, cols)
                gather_into(acc, jnp.dot(part, w[c0 : c0 + cols, pl.ds(n0, 256)], preferred_element_type=F32), p, n0)
            return 0

        lax.fori_loop(0, 3, pre, 0)
    slot_sent(0, 6)
    slot_got(0, 6)

    lane = lax.broadcasted_iota(jnp.int32, (128, 128), 1)
    row = lax.broadcasted_iota(jnp.int32, (128, 128), 0)
    spread = jnp.where((row < 8) & (lane < 32) & (lane % 8 == row), 1.0, 0.0).astype(BF16)

    for start, count, at in pieces(1):
        extra = rw[start // 128]
        route = jnp.dot(extra, spread, preferred_element_type=F32)
        taken = jnp.where((route == own) & (lane >= 8), extra.astype(F32), 0.0)
        wcol[at] = jnp.broadcast_to(jnp.sum(taken, axis=1, keepdims=True), (128, 128)).reshape(4, 4, 8, 128)
        rep[at] = route.reshape(4, 4, 8, 128)

    def activate(i, _):
        k, y = i // 4, i % 4
        g, u = ag[k, y].reshape(32, 768), au[k, y].reshape(32, 768)
        w = wcol[k, y].reshape(32, 128)[:, 0:1]
        s = jax.nn.sigmoid(g)
        silu = g * s * w
        hidden = silu * u
        ah[k, y] = hidden.reshape(4, 8, 768)
        hw[0][pl.ds(pl.multiple_of(i * 32, 32), 32), :] = hidden.astype(BF16)
        ag[k, y] = (u * s * w * (1.0 + g * (1.0 - s))).reshape(4, 8, 768)
        au[k, y] = silu.reshape(4, 8, 768)
        return 0

    lax.fori_loop(0, 32, activate, 0)

    def ordered(acc, out, p):
        for row, count, at in pieces(p):
            out[row : row + count, :] = acc[at].reshape(count, 768).astype(BF16)

    for p, (_, _, _, c0, cols) in enumerate(PARTS):
        if p:
            ordered(ah, hw[p], p)

        def forward(n0, width, p=p, c0=c0):
            r = jnp.dot(hw[p][...], wd[:, pl.ds(c0 + n0, width)], preferred_element_type=F32)
            send[p][:, :, pl.ds(n0, width)] = r.astype(BF16).reshape(8, 128, width)

        tiles(cols, forward)
        slot_start(1, send[p], xb[p], p, p)

    for p in (2, 1, 0):
        c0, cols = PARTS[p][3:]
        slot_sent(0, 3 + p)
        slot_got(0, 3 + p)

        def hidden_back(n, _, p=p, c0=c0, cols=cols):
            n0 = pl.multiple_of(n * 256, 256)
            r = contract(c[p][...].reshape(1024, cols), wd[pl.ds(n0, 256), c0 : c0 + cols], 1, 1)
            gather_into(ah, r, p, n0)
            return 0

        lax.fori_loop(0, 3, hidden_back, 0)
    lane32 = lax.broadcasted_iota(jnp.int32, (32, 128), 1)

    def derive(i, _):
        k, y = i // 4, i % 4
        at = pl.ds(pl.multiple_of(i * 32, 32), 32)
        h = ah[k, y].reshape(32, 768)
        gate, up = h * ag[k, y].reshape(32, 768), h * au[k, y].reshape(32, 768)
        ag[k, y], au[k, y] = gate.reshape(4, 8, 768), up.reshape(4, 8, 768)
        gb[at, :], ub[at, :] = gate.astype(BF16), up.astype(BF16)
        w = wcol[k, y].reshape(32, 128)
        value = jnp.sum(hw[0][at, :].astype(F32) * h, axis=1, keepdims=True) / w
        high = value.astype(BF16).astype(F32)
        both = jnp.where(lane32 < 8, high, jnp.where(lane32 < 16, value - high, 0.0))
        rep[k, y] = jnp.where(rep[k, y].reshape(32, 128) == own, both, 0.0).reshape(4, 8, 128)
        return 0

    lax.fori_loop(0, 32, derive, 0)
    for start, count, at in pieces(1):
        send[6][start // 128] = rep[at].reshape(128, 128).astype(BF16)
    slot_start(1, send[6], vr, 1, 6)
    for p, (_, _, _, c0, cols) in enumerate(PARTS):
        if p:
            ordered(ag, gb, p)
            ordered(au, ub, p)

        def backward(n0, width, p=p, c0=c0):
            at = pl.ds(c0 + n0, width)
            r = contract(gb[...], wg[at, :], 1, 1) + contract(ub[...], wu[at, :], 1, 1)
            send[3 + p][:, :, pl.ds(n0, width)] = r.astype(BF16).reshape(8, 128, width)

        tiles(cols, backward)
        slot_start(1, send[3 + p], cb[p], p, 3 + p)

    sent = []
    back_in = [*xb, *cb, vr]

    def go(copy):
        copy.start()
        sent.append(copy)

    def ring_copy(p, n, chunk, kind):
        a2 = PARTS[p][1]
        target = device(moved(co, a2, (co[a2] + (1 if kind in (0, 2, 3) else 3)) % 4), core)
        return remote(send[n].at[chunk], ring[n].at[kind], s5.at[n, kind], r5.at[n, kind], target)

    def ring_first(p, n):
        slot_sent(1, n)
        slot_got(1, n)
        cols = send[n].shape[-1]
        me = co[PARTS[p][1]]
        for d in (2, 1, 3, 0):
            g = (me + d) % 4
            got = back_in[n][:, pl.ds(pl.multiple_of(g * 32, 32), 32), :].reshape(256, cols)
            r = jnp.dot(st[p, g], got, preferred_element_type=F32)
            send[n][pl.ds(2 * g, 2)] = r.astype(BF16).reshape(2, 128, cols)
            if d == 2:
                go(ring_copy(p, n, 2 * g, 0))
                go(ring_copy(p, n, 2 * g + 1, 1))
            if d == 1:
                go(ring_copy(p, n, 2 * g + 1, 3))
            if d == 3:
                go(ring_copy(p, n, 2 * g, 4))

    def stage(i, cols):
        return hw[0].at[128 * i : 128 * i + 128, 0:cols]

    def ring_pass(items):
        todo = []
        for i, (p, n) in enumerate(items):
            me = co[PARTS[p][1]]
            cols = send[n].shape[-1]
            for j, (chunk, out) in enumerate(((2 * ((me + 1) % 4), 2), (2 * ((me + 3) % 4) + 1, 5))):
                ring_copy(p, n, chunk, j).wait_recv()
                slot = 2 * i + j
                copy = pltpu.make_async_copy(ring[n].at[j], stage(slot, cols), ls.at[slot])
                copy.start()
                todo.append((p, n, chunk, out, copy, stage(slot, cols)))
        for p, n, chunk, out, copy, held in todo:
            copy.wait()
            send[n][chunk] = (send[n][chunk].astype(F32) + held[...].astype(F32)).astype(BF16)
            go(ring_copy(p, n, chunk, out))

    def line_first(items):
        todo = []

        def finish(p, n, copies):
            a1, a2 = PARTS[p][:2]
            for h in (0, 1):
                chunk = 2 * co[a2] + h
                total = send[n][chunk].astype(F32)
                for copy, held in copies[h]:
                    copy.wait()
                    total = total + held[...].astype(F32)
                send[n][chunk] = total.astype(BF16)
            for d in (2, 1, 3):
                i = (co[a1] + d) % 4
                chunk, at = source(p, co[a2], i)
                go(remote(
                    send[n].at[chunk, at], line[n].at[co[a1]], s6.at[n, d - 1], r6.at[n, co[a1]],
                    device(moved(co, a1, i), core),
                ))
            chunk, at = source(p, co[a2], co[a1])
            mine = pltpu.make_async_copy(send[n].at[chunk, at], line[n].at[co[a1]], s6.at[n, 3])
            mine.start()
            owns.append(mine)

        for i, (p, n) in enumerate(items):
            cols = send[n].shape[-1]
            copies = ([], [])
            for kind in (2, 3, 4, 5):
                ring_copy(p, n, 0, kind).wait_recv()
                slot = 4 * (i % 2) + kind - 2
                copy = pltpu.make_async_copy(ring[n].at[kind], stage(slot, cols), ls.at[slot])
                copy.start()
                copies[kind % 2].append((copy, stage(slot, cols)))
            todo.append((p, n, copies))
            if i:
                finish(*todo[i - 1])
        finish(*todo[-1])

    owns = []
    outs = [(p, p) for p in range(3)]
    backs = [(1, 6)] + [(p, 3 + p) for p in range(3)]
    for item in outs:
        ring_first(*item)
    for p, (_, _, _, c0, cols) in enumerate(PARTS):

        def down(n, _, p=p, c0=c0, cols=cols):
            at = pl.ds(pl.multiple_of(n * 256, 256), 256)
            wd[at, c0 : c0 + cols] = contract(hw[p][:, at], c[p][...].reshape(1024, cols), 0, 0).astype(BF16)
            return 0

        lax.fori_loop(0, 3, down, 0)

    def weight_grads(p):
        c0, cols = PARTS[p][3:]

        def gate(n0, width):
            part = x[p][:, :, pl.ds(n0, width)].reshape(1024, width)
            at = pl.ds(c0 + n0, width)
            wg[at, :] = contract(part, gb[...], 0, 0).astype(BF16)
            wu[at, :] = contract(part, ub[...], 0, 0).astype(BF16)

        tiles(cols, gate)

    weight_grads(2)
    for item in backs:
        ring_first(*item)
    ordered(ag, gb, 1)
    ordered(au, ub, 1)
    weight_grads(1)
    ring_pass(outs)
    ordered(ag, gb, 0)
    ordered(au, ub, 0)
    weight_grads(0)
    ring_pass(backs)
    line_first(outs)
    line_first(backs)
    for p, n in outs + backs:
        a1 = PARTS[p][0]
        for d in (1, 2, 3):
            j = (co[a1] + d) % 4
            got = line[n].at[j]
            remote(got, got, s6.at[n, d - 1], r6.at[n, j], device(moved(co, a1, j), core)).wait_recv()
    for copy in sent:
        copy.wait_send()
    for copy in owns:
        copy.wait()


def last_kernel(*refs):
    line, grads, outs = refs[0:7], refs[7:10], refs[10:16]
    held, mixed, tgrad, vgrad = refs[16:20]
    ls, hs, os = refs[20:23]
    copies = []
    for i in range(3):
        part = grads[i].shape[0] // 4
        for j in range(4):
            at = pl.ds(j * part, part)
            copies.append(pltpu.make_async_copy(grads[i].at[at], outs[3 + i].at[at], hs.at[i, j]))
    spans = [(c0, cols) for _, _, _, c0, cols in PARTS]
    places = [(0, *span) for span in spans] + [(1, *span) for span in spans] + [(2, 0, 128)]
    loads = [
        pltpu.make_async_copy(line[n], held.at[a, :, :, pl.ds(c0, cols)], ls.at[n])
        for n, (a, c0, cols) in enumerate(places)
    ]
    for load in loads + copies:
        load.start()
    for load in loads:
        load.wait()

    def total(a, at):
        return jnp.sum(held[a, :, at, :].astype(F32), axis=0)

    def step(i, _):
        at = pl.ds(pl.multiple_of(i * 16, 16), 16)
        mixed[at, :] = total(0, at).astype(BF16)
        tgrad[at, :] = total(1, at).astype(BF16)
        return 0

    lax.fori_loop(0, 4, step, 0)
    lane = lax.broadcasted_iota(jnp.int32, (8, 128), 1)
    row = lax.broadcasted_iota(jnp.int32, (8, 128), 0)
    both = jnp.where((lane < 16) & (lane % 8 == row), 1.0, 0.0).astype(BF16)
    value = jnp.sum(held[2, :, :, 0:128].astype(F32), axis=0).astype(BF16)
    vgrad[...] = contract(both, value, 1, 1)
    ends = [pltpu.make_async_copy(src, dst, os.at[i]) for i, (src, dst) in enumerate(zip((mixed, tgrad, vgrad), outs[:3], strict=True))]
    for copy in ends:
        copy.start()
    for copy in ends + copies:
        copy.wait()


def per_device(tokens, routes, route_weights, cotangent, gate_weight, up_weight, down_weight):
    widths = [part[4] for part in PARTS]
    shape, dma = jax.ShapeDtypeStruct, pltpu.SemaphoreType.DMA
    any_, vmem = pl.BlockSpec(memory_space=pl.ANY), pl.BlockSpec(memory_space=pltpu.VMEM)
    items = widths * 2 + [128]
    weight_shapes = [shape((2048, 768), BF16), shape((2048, 768), BF16), shape((768, 2048), BF16)]

    def chunks(ws):
        return [pltpu.VMEM((8, 128, w), BF16) for w in ws]

    got = pl.pallas_call(
        moe_kernel,
        out_shape=[pltpu.VMEM(w.shape, BF16) for w in weight_shapes] + [shape((6, 128, w), BF16) for w in items] + [shape((4, 64, w), BF16) for w in items],
        in_specs=[vmem] * 4 + [any_] * 3,
        out_specs=[vmem] * 3 + [any_] * 14,
        scratch_shapes=chunks(widths * 2 + [128] * 5)
        + chunks(items)
        + chunks(items)
        + [pltpu.VMEM((3, 4, 256, 256), BF16)]
        + [pltpu.VMEM((8, 4, 4, 8, 768), F32)] * 3
        + [pltpu.VMEM((1024, 768), BF16)] * 5
        + [pltpu.VMEM((8, 4, 4, 8, 128), F32)] * 2
        + [dma((10, 3)), dma((10, 4)), dma((10, 6)), dma((10, 4, 2)), dma((7, 8)), dma((7, 8)), dma((7,)), dma((3,))]
        + [dma((7, 8)), dma((7, 8)), dma((7,)), dma((7, 6)), dma((7, 6)), dma((7, 4)), dma((7, 4)), dma((8,))],
        compiler_params=pltpu.CompilerParams(collective_id=0, has_side_effects=True, vmem_limit_bytes=53 * 2**20),
    )(tokens, cotangent, routes.T, route_weights.T, gate_weight[0], up_weight[0], down_weight[0])
    mixed, token_grad, weight_grad, gate_grad, up_grad, down_grad = pl.pallas_call(
        last_kernel,
        out_shape=[shape((64, 2048), BF16), shape((64, 2048), BF16), shape((8, 64), F32)] + weight_shapes,
        in_specs=[any_] * 10,
        out_specs=[any_] * 6,
        scratch_shapes=[
            pltpu.VMEM((3, 4, 64, 2048), BF16),
            pltpu.VMEM((64, 2048), BF16),
            pltpu.VMEM((64, 2048), BF16),
            pltpu.VMEM((8, 64), F32),
            dma((7,)),
            dma((3, 4)),
            dma((3,)),
        ],
        compiler_params=pltpu.CompilerParams(vmem_limit_bytes=16 * 2**20),
    )(*[pltpu.with_memory_space_constraint(g, pltpu.HBM) for g in got[10:17]], *[pltpu.with_memory_space_constraint(g, pltpu.VMEM) for g in got[0:3]])
    return (mixed, token_grad, weight_grad.T, gate_grad[None], up_grad[None], down_grad[None])


def solution(mesh):
    placed = (
        P(("node", "rail"), None),
        P(("node", "rail"), None),
        P(("node", "rail"), None),
        P(("node", "rail"), None),
        P(("node", "rail"), None, None),
        P(("node", "rail"), None, None),
        P(("node", "rail"), None, None),
    )
    return jax.shard_map(
        per_device,
        mesh=mesh,
        in_specs=placed,
        out_specs=(
            P(("node", "rail"), None),
            P(("node", "rail"), None),
            P(("node", "rail"), None),
            P(("node", "rail"), None, None),
            P(("node", "rail"), None, None),
            P(("node", "rail"), None, None),
        ),
        check_vma=False,
    )
```

```python
import jax
import jax.numpy as jnp
from jax import lax
from jax.experimental import pallas as pl
from jax.experimental.pallas import tpu as pltpu
from jax.sharding import PartitionSpec as P

MESH = pl.DeviceIdType.MESH
F32, BF16 = jnp.float32, jnp.bfloat16
PARTS = ((0, 1, 2, 0, 768), (1, 2, 0, 768, 640), (2, 0, 1, 1408, 640))


def place():
    node, rail = lax.axis_index("node"), lax.axis_index("rail")
    return (node // 2, rail % 4, rail // 4), node % 2


def moved(co, axis, value):
    return tuple(value if i == axis else v for i, v in enumerate(co))


def device(co, core):
    return (co[0] * 2 + core, co[2] * 4 + co[1])


def remote(src, dst, send, recv, target):
    return pltpu.make_async_remote_copy(
        src_ref=src, dst_ref=dst, send_sem=send, recv_sem=recv, device_id=target, device_id_type=MESH
    )


def greet(co, core):
    barrier = pltpu.get_barrier_semaphore()
    targets = [device(co, 1 - core)]
    for axis in range(3):
        for step in (1, 2, 3):
            there = moved(co, axis, (co[axis] + step) % 4)
            targets += [device(there, core), device(there, 1 - core)]
    for target in targets:
        pl.semaphore_signal(barrier, inc=1, device_id=target, device_id_type=MESH)
    return barrier, len(targets)


def one_hot(table, co, slot_axis):
    expert = lax.broadcasted_iota(jnp.int32, (128, 256), 0)
    lane = lax.broadcasted_iota(jnp.int32, (128, 256), 1)
    core, along = lane // 128, (lane // 32) % 4
    there = moved(co, slot_axis, along)
    owner = (there[0] * 2 + core) * 16 + there[2] * 4 + there[1]
    spread = jnp.dot(table, jnp.where(expert == owner, 1.0, 0.0).astype(BF16), preferred_element_type=F32)
    row = lax.broadcasted_iota(jnp.int32, (256, 256), 0)
    lane = lax.broadcasted_iota(jnp.int32, (256, 256), 1)
    wanted = jnp.where(row // 64 == (lane // 8) % 4, lane % 8 + 1, -1).astype(F32)
    return jnp.where(spread == wanted, 1.0, 0.0).astype(BF16)


def pieces(p):
    for k in range(8):
        c, d = k // 4, k % 4
        if p == 0:
            yield k * 128, 128, (k,)
        elif p == 1:
            yield k * 128, 128, (slice(4 * c, 4 * c + 4), slice(None), d)
        else:
            for x in range(4):
                yield k * 128 + x * 32, 32, (slice(4 * c, 4 * c + 4), d, x)


def tiles(cols, body):
    def step(n, _):
        body(pl.multiple_of(n * 256, 256), 256)
        return 0

    lax.fori_loop(0, cols // 256, step, 0)
    if cols % 256:
        body(cols - cols % 256, cols % 256)


def contract(a, b, da, db):
    return lax.dot_general(a, b, (((da,), (db,)), ((), ())), preferred_element_type=F32)


def route_tables(routes, weights):
    lanes = lax.broadcasted_iota(jnp.int32, (64, 128), 1).astype(F32)
    ids = routes.astype(F32).astype(BF16)
    rows8 = lax.broadcasted_iota(jnp.int32, (8, 128), 0)
    named = jnp.zeros((64, 128), F32)
    for k in range(8):
        pick = jnp.where(rows8 == k, 1.0, 0.0).astype(BF16)
        named = named + jnp.where(contract(ids, pick, 0, 0) == lanes, 1.0, 0.0)
    row = lax.broadcasted_iota(jnp.int32, (64, 64), 0)
    col = lax.broadcasted_iota(jnp.int32, (64, 64), 1)
    upto = jnp.where(col <= row, 1.0, 0.0).astype(BF16)
    counted = jnp.dot(upto, named.astype(BF16), preferred_element_type=F32)
    table = (counted * named).astype(BF16)
    high = weights.astype(BF16)
    mid = (weights - high.astype(F32)).astype(BF16)
    low = (weights - high.astype(F32) - mid.astype(F32)).astype(BF16)
    lane8 = lax.broadcasted_iota(jnp.int32, (8, 128), 1)
    extra = jnp.zeros((64, 128), F32)
    for i, part in enumerate(((routes + 1).astype(F32).astype(BF16), high, mid, low)):
        extra = extra + contract(part, jnp.where(lane8 == rows8 + 8 * i, 1.0, 0.0).astype(BF16), 0, 0)
    return table, extra.astype(BF16)


def moe_kernel(tok, cot, routes, weights, wgi, wui, wdi, *refs):
    wg, wu, wd = refs[0:3]
    ring, line = refs[3:10], refs[10:17]
    refs = refs[17:]
    xb, cb, vr, qb, rwb = refs[0:3], refs[3:6], refs[6], refs[7:10], refs[10]
    send = refs[11:18]
    x, c, rw, st = refs[18:21], refs[21:24], refs[24], refs[25]
    ag, au, ah = refs[26:29]
    hw, gb, ub, wcol, rep = refs[29:32], refs[32], refs[33], refs[34], refs[35]
    s1, r1, s2, r2, s3, r3, loc3, ld, s4, r4, loc4, s5, r5, s6, r6, ls = refs[36:52]
    co, core = place()
    own = ((co[0] * 2 + core) * 16 + co[2] * 4 + co[1] + 1).astype(F32)
    barrier, count = greet(co, core)
    loads = [pltpu.make_async_copy(src, dst, ld.at[i]) for i, (src, dst) in enumerate(((wgi, wg), (wui, wu), (wdi, wd)))]

    def half_rows(i):
        return pl.ds(pl.multiple_of((i % 2) * 64, 64), 64)

    def source(p, i2, i1):
        return 2 * i2 + i1 // 2, half_rows(i1)

    rows = [(xb[p], p, p) for p in range(3)]
    grads = [(cb[p], p, 3 + p) for p in range(3)]
    tables = [(qb[p], p, 6 + p) for p in range(3)] + [(rwb, 1, 9)]

    def put(buf, p, value):
        a1, a2 = PARTS[p][:2]
        chunk, at = source(p, co[a2], co[a1])
        buf[chunk, at] = value

    flying = {}

    def launch(n, copies):
        for copy in copies:
            copy.start()
        flying.setdefault(n, []).extend(copies)

    def landed(n):
        for copy in flying.pop(n):
            copy.wait_send()

    def first_start(buf, p, n):
        a1, a2 = PARTS[p][:2]
        chunk, at = source(p, co[a2], co[a1])
        mine = buf.at[chunk, at]
        launch(n, [
            remote(mine, mine, s1.at[n, d - 1], r1.at[n, co[a1]], device(moved(co, a1, (co[a1] + d) % 4), core))
            for d in (2, 1, 3)
        ])

    def first_wait(buf, p, n):
        a1, a2 = PARTS[p][:2]
        for d in (1, 2, 3):
            i = (co[a1] + d) % 4
            chunk, at = source(p, co[a2], i)
            got = buf.at[chunk, at]
            remote(got, got, s1.at[n, d - 1], r1.at[n, i], device(moved(co, a1, i), core)).wait_recv()

    def second_copy(buf, p, n, block, h, right, number):
        a2 = PARTS[p][1]
        part = buf.at[2 * block + h]
        target = device(moved(co, a2, (co[a2] + (1 if right else 3)) % 4), core)
        return remote(part, part, s2.at[n, number], r2.at[n, block, h], target)

    def second_start(buf, p, n):
        me = co[PARTS[p][1]]
        launch(n, [
            second_copy(buf, p, n, me, 0, True, 0),
            second_copy(buf, p, n, me, 1, False, 1),
            second_copy(buf, p, n, me, 1, True, 2),
            second_copy(buf, p, n, me, 0, False, 3),
        ])

    def second_wait(buf, p, n, d, h):
        second_copy(buf, p, n, (co[PARTS[p][1]] + d) % 4, h, True, 0).wait_recv()

    def relay(buf, p, n):
        me = co[PARTS[p][1]]
        second_wait(buf, p, n, 3, 0)
        launch(n, [second_copy(buf, p, n, (me + 3) % 4, 0, True, 4)])
        second_wait(buf, p, n, 1, 1)
        launch(n, [second_copy(buf, p, n, (me + 1) % 4, 1, False, 5)])

    def near_wait(buf, p, n):
        second_wait(buf, p, n, 3, 1)
        second_wait(buf, p, n, 1, 0)

    def far_wait(buf, p, n):
        second_wait(buf, p, n, 2, 0)
        second_wait(buf, p, n, 2, 1)

    def build(p, d):
        g = (co[PARTS[p][1]] + d) % 4
        st[p, g] = one_hot(qb[p][pl.ds(2 * g, 2)].reshape(256, 128), co, PARTS[p][2])

    def pick(buf, out, p, d):
        cols = buf.shape[-1]
        g = (co[PARTS[p][1]] + d) % 4
        r = contract(st[p, g], buf[pl.ds(2 * g, 2)].reshape(256, cols), 0, 0)
        out[:, pl.ds(pl.multiple_of(g * 32, 32), 32), :] = r.astype(BF16).reshape(8, 32, cols)

    for p, (_, _, _, c0, cols) in enumerate(PARTS):
        put(xb[p], p, tok[:, c0 : c0 + cols])
    pl.semaphore_wait(barrier, count)
    for item in rows:
        first_start(*item)
    table, extra = route_tables(routes[...], weights[...])
    for p in range(3):
        put(qb[p], p, table)
    put(rwb, 1, extra)
    for item in tables:
        first_start(*item)
    for p, (_, _, _, c0, cols) in enumerate(PARTS):
        put(cb[p], p, cot[:, c0 : c0 + cols])
    for item in grads:
        first_start(*item)
    for load in loads:
        load.start()
    for item in rows + tables + grads:
        first_wait(*item)
        second_start(*item)
    def slot_ends(p):
        axis = PARTS[p][2]
        for dc in (0, 1):
            for d in (2, 1, 3, 0):
                if dc == 0 and d == 0:
                    continue
                there, other = (co[axis] + d) % 4, (core + dc) % 2
                yield dc * 4 + d, other * 4 + there, device(moved(co, axis, there), other)

    moving = {}

    def slot_start(way, src, dst, p, n):
        me = core * 4 + co[PARTS[p][2]]
        ss, rs, loc = (s3, r3, loc3) if way == 0 else (s4, r4, loc4)
        copies = [remote(src.at[k], dst.at[me], ss.at[n, i], rs.at[n, me], to) for i, k, to in slot_ends(p)]
        for copy in copies:
            copy.start()
        local = pltpu.make_async_copy(src.at[me], dst.at[me], loc.at[n])
        local.start()
        moving[way, n] = (src, dst, p, copies, local, ss, rs)

    def slot_sent(way, n):
        for copy in moving[way, n][3]:
            copy.wait_send()
        moving[way, n][4].wait()

    def slot_got(way, n):
        src, dst, p, _, _, ss, rs = moving[way, n]
        for i, k, to in slot_ends(p):
            remote(src.at[k], dst.at[k], ss.at[n, i], rs.at[n, k], to).wait_recv()

    for p in range(3):
        build(p, 0)
    pick(rwb, send[6], 1, 0)
    for p in range(3):
        pick(xb[p], send[p], p, 0)
    for item in rows + tables + grads:
        relay(*item)
    for item in tables:
        near_wait(*item)
    for p in range(3):
        build(p, 1)
        build(p, 3)
    for p in range(3):
        near_wait(*rows[p])
        pick(xb[p], send[p], p, 1)
        pick(xb[p], send[p], p, 3)
    pick(rwb, send[6], 1, 1)
    pick(rwb, send[6], 1, 3)
    for item in tables:
        far_wait(*item)
    for p in range(3):
        build(p, 2)
    for p in range(3):
        far_wait(*rows[p])
        pick(xb[p], send[p], p, 2)
        landed(p)
        slot_start(0, send[p], x[p], p, p)
    pick(rwb, send[6], 1, 2)
    slot_start(0, send[6], rw, 1, 6)
    for p in range(3):
        near_wait(*grads[p])
        for d in (0, 1, 3):
            pick(cb[p], send[3 + p], p, d)
    for p in range(3):
        far_wait(*grads[p])
        pick(cb[p], send[3 + p], p, 2)
        landed(3 + p)
        slot_start(0, send[3 + p], c[p], p, 3 + p)
    for n in range(6, 10):
        landed(n)

    for load in loads:
        load.wait()

    def gather_into(acc, r, p, n0):
        for row, count, at in pieces(p):
            at = (*at, *([slice(None)] * (4 - len(at))), pl.ds(n0, 256))
            where = acc.at[at]
            piece = r[row : row + count].reshape(where.shape)
            where[...] = piece if p == 2 else where[...] + piece

    for p in (2, 1, 0):
        c0, cols = PARTS[p][3:]
        slot_sent(0, p)
        slot_got(0, p)

        def pre(n, _, p=p, c0=c0, cols=cols):
            n0 = pl.multiple_of(n * 256, 256)
            for w, acc in ((wg, ag), (wu, au)):
                part = x[p][...].reshape(1024, cols)
                gather_into(acc, jnp.dot(part, w[c0 : c0 + cols, pl.ds(n0, 256)], preferred_element_type=F32), p, n0)
            return 0

        lax.fori_loop(0, 3, pre, 0)
    slot_sent(0, 6)
    slot_got(0, 6)

    lane = lax.broadcasted_iota(jnp.int32, (128, 128), 1)
    row = lax.broadcasted_iota(jnp.int32, (128, 128), 0)
    spread = jnp.where((row < 8) & (lane < 32) & (lane % 8 == row), 1.0, 0.0).astype(BF16)

    for start, count, at in pieces(1):
        extra = rw[start // 128]
        route = jnp.dot(extra, spread, preferred_element_type=F32)
        taken = jnp.where((route == own) & (lane >= 8), extra.astype(F32), 0.0)
        wcol[at] = jnp.broadcast_to(jnp.sum(taken, axis=1, keepdims=True), (128, 128)).reshape(4, 4, 8, 128)
        rep[at] = route.reshape(4, 4, 8, 128)

    def activate(i, _):
        k, y = i // 4, i % 4
        g, u = ag[k, y].reshape(32, 768), au[k, y].reshape(32, 768)
        w = wcol[k, y].reshape(32, 128)[:, 0:1]
        s = jax.nn.sigmoid(g)
        silu = g * s * w
        hidden = silu * u
        ah[k, y] = hidden.reshape(4, 8, 768)
        hw[0][pl.ds(pl.multiple_of(i * 32, 32), 32), :] = hidden.astype(BF16)
        ag[k, y] = (u * s * w * (1.0 + g * (1.0 - s))).reshape(4, 8, 768)
        au[k, y] = silu.reshape(4, 8, 768)
        return 0

    lax.fori_loop(0, 32, activate, 0)

    def ordered(acc, out, p):
        for row, count, at in pieces(p):
            out[row : row + count, :] = acc[at].reshape(count, 768).astype(BF16)

    for p, (_, _, _, c0, cols) in enumerate(PARTS):
        if p:
            ordered(ah, hw[p], p)

        def forward(n0, width, p=p, c0=c0):
            r = jnp.dot(hw[p][...], wd[:, pl.ds(c0 + n0, width)], preferred_element_type=F32)
            send[p][:, :, pl.ds(n0, width)] = r.astype(BF16).reshape(8, 128, width)

        tiles(cols, forward)
        slot_start(1, send[p], xb[p], p, p)

    for p in (2, 1, 0):
        c0, cols = PARTS[p][3:]
        slot_sent(0, 3 + p)
        slot_got(0, 3 + p)

        def hidden_back(n, _, p=p, c0=c0, cols=cols):
            n0 = pl.multiple_of(n * 256, 256)
            r = contract(c[p][...].reshape(1024, cols), wd[pl.ds(n0, 256), c0 : c0 + cols], 1, 1)
            gather_into(ah, r, p, n0)
            return 0

        lax.fori_loop(0, 3, hidden_back, 0)
    lane32 = lax.broadcasted_iota(jnp.int32, (32, 128), 1)

    def derive(i, _):
        k, y = i // 4, i % 4
        at = pl.ds(pl.multiple_of(i * 32, 32), 32)
        h = ah[k, y].reshape(32, 768)
        gate, up = h * ag[k, y].reshape(32, 768), h * au[k, y].reshape(32, 768)
        ag[k, y], au[k, y] = gate.reshape(4, 8, 768), up.reshape(4, 8, 768)
        gb[at, :], ub[at, :] = gate.astype(BF16), up.astype(BF16)
        w = wcol[k, y].reshape(32, 128)
        value = jnp.sum(hw[0][at, :].astype(F32) * h, axis=1, keepdims=True) / w
        high = value.astype(BF16).astype(F32)
        both = jnp.where(lane32 < 8, high, jnp.where(lane32 < 16, value - high, 0.0))
        rep[k, y] = jnp.where(rep[k, y].reshape(32, 128) == own, both, 0.0).reshape(4, 8, 128)
        return 0

    lax.fori_loop(0, 32, derive, 0)
    for start, count, at in pieces(1):
        send[6][start // 128] = rep[at].reshape(128, 128).astype(BF16)
    slot_start(1, send[6], vr, 1, 6)
    for p, (_, _, _, c0, cols) in enumerate(PARTS):
        if p:
            ordered(ag, gb, p)
            ordered(au, ub, p)

        def backward(n0, width, p=p, c0=c0):
            at = pl.ds(c0 + n0, width)
            r = contract(gb[...], wg[at, :], 1, 1) + contract(ub[...], wu[at, :], 1, 1)
            send[3 + p][:, :, pl.ds(n0, width)] = r.astype(BF16).reshape(8, 128, width)

        tiles(cols, backward)
        slot_start(1, send[3 + p], cb[p], p, 3 + p)

    sent = []
    back_in = [*xb, *cb, vr]

    def go(copy):
        copy.start()
        sent.append(copy)

    def ring_copy(p, n, chunk, kind):
        a2 = PARTS[p][1]
        target = device(moved(co, a2, (co[a2] + (1 if kind in (0, 2, 3) else 3)) % 4), core)
        return remote(send[n].at[chunk], ring[n].at[kind], s5.at[n, kind], r5.at[n, kind], target)

    def ring_first(p, n):
        slot_sent(1, n)
        slot_got(1, n)
        cols = send[n].shape[-1]
        me = co[PARTS[p][1]]
        for d in (2, 1, 3, 0):
            g = (me + d) % 4
            got = back_in[n][:, pl.ds(pl.multiple_of(g * 32, 32), 32), :].reshape(256, cols)
            r = jnp.dot(st[p, g], got, preferred_element_type=F32)
            send[n][pl.ds(2 * g, 2)] = r.astype(BF16).reshape(2, 128, cols)
            if d == 2:
                go(ring_copy(p, n, 2 * g, 0))
                go(ring_copy(p, n, 2 * g + 1, 1))
            if d == 1:
                go(ring_copy(p, n, 2 * g + 1, 3))
            if d == 3:
                go(ring_copy(p, n, 2 * g, 4))

    def stage(i, cols):
        return hw[0].at[128 * i : 128 * i + 128, 0:cols]

    def ring_pass(items):
        todo = []
        for i, (p, n) in enumerate(items):
            me = co[PARTS[p][1]]
            cols = send[n].shape[-1]
            for j, (chunk, out) in enumerate(((2 * ((me + 1) % 4), 2), (2 * ((me + 3) % 4) + 1, 5))):
                ring_copy(p, n, chunk, j).wait_recv()
                slot = 2 * i + j
                copy = pltpu.make_async_copy(ring[n].at[j], stage(slot, cols), ls.at[slot])
                copy.start()
                todo.append((p, n, chunk, out, copy, stage(slot, cols)))
        for p, n, chunk, out, copy, held in todo:
            copy.wait()
            send[n][chunk] = (send[n][chunk].astype(F32) + held[...].astype(F32)).astype(BF16)
            go(ring_copy(p, n, chunk, out))

    def line_first(items):
        todo = []

        def finish(p, n, copies):
            a1, a2 = PARTS[p][:2]
            for h in (0, 1):
                chunk = 2 * co[a2] + h
                total = send[n][chunk].astype(F32)
                for copy, held in copies[h]:
                    copy.wait()
                    total = total + held[...].astype(F32)
                send[n][chunk] = total.astype(BF16)
            for d in (2, 1, 3):
                i = (co[a1] + d) % 4
                chunk, at = source(p, co[a2], i)
                go(remote(
                    send[n].at[chunk, at], line[n].at[co[a1]], s6.at[n, d - 1], r6.at[n, co[a1]],
                    device(moved(co, a1, i), core),
                ))
            chunk, at = source(p, co[a2], co[a1])
            mine = pltpu.make_async_copy(send[n].at[chunk, at], line[n].at[co[a1]], s6.at[n, 3])
            mine.start()
            owns.append(mine)

        for i, (p, n) in enumerate(items):
            cols = send[n].shape[-1]
            copies = ([], [])
            for kind in (2, 3, 4, 5):
                ring_copy(p, n, 0, kind).wait_recv()
                slot = 4 * (i % 2) + kind - 2
                copy = pltpu.make_async_copy(ring[n].at[kind], stage(slot, cols), ls.at[slot])
                copy.start()
                copies[kind % 2].append((copy, stage(slot, cols)))
            todo.append((p, n, copies))
            if i:
                finish(*todo[i - 1])
        finish(*todo[-1])

    owns = []
    outs = [(p, p) for p in range(3)]
    backs = [(1, 6)] + [(p, 3 + p) for p in range(3)]
    for item in outs:
        ring_first(*item)
    for p, (_, _, _, c0, cols) in enumerate(PARTS):

        def down(n, _, p=p, c0=c0, cols=cols):
            at = pl.ds(pl.multiple_of(n * 256, 256), 256)
            wd[at, c0 : c0 + cols] = contract(hw[p][:, at], c[p][...].reshape(1024, cols), 0, 0).astype(BF16)
            return 0

        lax.fori_loop(0, 3, down, 0)

    def weight_grads(p):
        c0, cols = PARTS[p][3:]

        def gate(n0, width):
            part = x[p][:, :, pl.ds(n0, width)].reshape(1024, width)
            at = pl.ds(c0 + n0, width)
            wg[at, :] = contract(part, gb[...], 0, 0).astype(BF16)
            wu[at, :] = contract(part, ub[...], 0, 0).astype(BF16)

        tiles(cols, gate)

    weight_grads(2)
    ordered(ag, gb, 1)
    ordered(au, ub, 1)
    weight_grads(1)
    for item in backs:
        ring_first(*item)
    ring_pass(outs)
    ordered(ag, gb, 0)
    ordered(au, ub, 0)
    weight_grads(0)
    ring_pass(backs)
    line_first(outs)
    line_first(backs)
    for p, n in outs + backs:
        a1 = PARTS[p][0]
        for d in (1, 2, 3):
            j = (co[a1] + d) % 4
            got = line[n].at[j]
            remote(got, got, s6.at[n, d - 1], r6.at[n, j], device(moved(co, a1, j), core)).wait_recv()
    for copy in sent:
        copy.wait_send()
    for copy in owns:
        copy.wait()


def last_kernel(*refs):
    line, grads, outs = refs[0:7], refs[7:10], refs[10:16]
    held, mixed, tgrad, vgrad = refs[16:20]
    ls, hs, os = refs[20:23]
    copies = []
    for i in range(3):
        part = grads[i].shape[0] // 4
        for j in range(4):
            at = pl.ds(j * part, part)
            copies.append(pltpu.make_async_copy(grads[i].at[at], outs[3 + i].at[at], hs.at[i, j]))
    spans = [(c0, cols) for _, _, _, c0, cols in PARTS]
    places = [(0, *span) for span in spans] + [(1, *span) for span in spans] + [(2, 0, 128)]
    loads = [
        pltpu.make_async_copy(line[n], held.at[a, :, :, pl.ds(c0, cols)], ls.at[n])
        for n, (a, c0, cols) in enumerate(places)
    ]
    for load in loads + copies:
        load.start()
    for load in loads:
        load.wait()

    def total(a, at):
        return jnp.sum(held[a, :, at, :].astype(F32), axis=0)

    def step(i, _):
        at = pl.ds(pl.multiple_of(i * 16, 16), 16)
        mixed[at, :] = total(0, at).astype(BF16)
        tgrad[at, :] = total(1, at).astype(BF16)
        return 0

    lax.fori_loop(0, 4, step, 0)
    lane = lax.broadcasted_iota(jnp.int32, (8, 128), 1)
    row = lax.broadcasted_iota(jnp.int32, (8, 128), 0)
    both = jnp.where((lane < 16) & (lane % 8 == row), 1.0, 0.0).astype(BF16)
    value = jnp.sum(held[2, :, :, 0:128].astype(F32), axis=0).astype(BF16)
    vgrad[...] = contract(both, value, 1, 1)
    ends = [pltpu.make_async_copy(src, dst, os.at[i]) for i, (src, dst) in enumerate(zip((mixed, tgrad, vgrad), outs[:3], strict=True))]
    for copy in ends:
        copy.start()
    for copy in ends + copies:
        copy.wait()


def per_device(tokens, routes, route_weights, cotangent, gate_weight, up_weight, down_weight):
    widths = [part[4] for part in PARTS]
    shape, dma = jax.ShapeDtypeStruct, pltpu.SemaphoreType.DMA
    any_, vmem = pl.BlockSpec(memory_space=pl.ANY), pl.BlockSpec(memory_space=pltpu.VMEM)
    items = widths * 2 + [128]
    weight_shapes = [shape((2048, 768), BF16), shape((2048, 768), BF16), shape((768, 2048), BF16)]

    def chunks(ws):
        return [pltpu.VMEM((8, 128, w), BF16) for w in ws]

    got = pl.pallas_call(
        moe_kernel,
        out_shape=[pltpu.VMEM(w.shape, BF16) for w in weight_shapes] + [shape((6, 128, w), BF16) for w in items] + [shape((4, 64, w), BF16) for w in items],
        in_specs=[vmem] * 4 + [any_] * 3,
        out_specs=[vmem] * 3 + [any_] * 14,
        scratch_shapes=chunks(widths * 2 + [128] * 5)
        + chunks(items)
        + chunks(items)
        + [pltpu.VMEM((3, 4, 256, 256), BF16)]
        + [pltpu.VMEM((8, 4, 4, 8, 768), F32)] * 3
        + [pltpu.VMEM((1024, 768), BF16)] * 5
        + [pltpu.VMEM((8, 4, 4, 8, 128), F32)] * 2
        + [dma((10, 3)), dma((10, 4)), dma((10, 6)), dma((10, 4, 2)), dma((7, 8)), dma((7, 8)), dma((7,)), dma((3,))]
        + [dma((7, 8)), dma((7, 8)), dma((7,)), dma((7, 6)), dma((7, 6)), dma((7, 4)), dma((7, 4)), dma((8,))],
        compiler_params=pltpu.CompilerParams(collective_id=0, has_side_effects=True, vmem_limit_bytes=53 * 2**20),
    )(tokens, cotangent, routes.T, route_weights.T, gate_weight[0], up_weight[0], down_weight[0])
    mixed, token_grad, weight_grad, gate_grad, up_grad, down_grad = pl.pallas_call(
        last_kernel,
        out_shape=[shape((64, 2048), BF16), shape((64, 2048), BF16), shape((8, 64), F32)] + weight_shapes,
        in_specs=[any_] * 10,
        out_specs=[any_] * 6,
        scratch_shapes=[
            pltpu.VMEM((3, 4, 64, 2048), BF16),
            pltpu.VMEM((64, 2048), BF16),
            pltpu.VMEM((64, 2048), BF16),
            pltpu.VMEM((8, 64), F32),
            dma((7,)),
            dma((3, 4)),
            dma((3,)),
        ],
        compiler_params=pltpu.CompilerParams(vmem_limit_bytes=16 * 2**20),
    )(*[pltpu.with_memory_space_constraint(g, pltpu.HBM) for g in got[10:17]], *[pltpu.with_memory_space_constraint(g, pltpu.VMEM) for g in got[0:3]])
    return (mixed, token_grad, weight_grad.T, gate_grad[None], up_grad[None], down_grad[None])


def solution(mesh):
    placed = (
        P(("node", "rail"), None),
        P(("node", "rail"), None),
        P(("node", "rail"), None),
        P(("node", "rail"), None),
        P(("node", "rail"), None, None),
        P(("node", "rail"), None, None),
        P(("node", "rail"), None, None),
    )
    return jax.shard_map(
        per_device,
        mesh=mesh,
        in_specs=placed,
        out_specs=(
            P(("node", "rail"), None),
            P(("node", "rail"), None),
            P(("node", "rail"), None),
            P(("node", "rail"), None, None),
            P(("node", "rail"), None, None),
            P(("node", "rail"), None, None),
        ),
        check_vma=False,
    )
```
